32 devices in a mesh: groups: 2 (over y), row: 4 (over x, core), col: 4 (over z).
Axes of the slice: x: 2, y: 2, z: 4, core: 2. Of those that a mesh axis runs over, the one named last changes fastest.
Arguments:
- tokens: bfloat16 [128, 7168], P(('groups', 'row', 'col')), parts along dimension 0, may hold values from -6 to 6
- expert_ids: int32 [128, 8], P(('groups', 'row', 'col')), parts along dimension 0, may hold values from 0 to 15, all different within a row; in each aligned block of 4 rows (0 to 3, 4 to 7, ...) at most 3 rows name the same one
- route_weight: bfloat16 [128, 8], P(('groups', 'row', 'col')), parts along dimension 0, may hold values from 0.099609375 to 0.59765625
- dither: bfloat16 [128, 4, 7168], P(('groups', 'row', 'col')), parts along dimension 0, may hold values from 0 to 1
- gate_proj: bfloat16 [4, 4, 7168, 2048], P('row', 'col'), may hold values from -0.0625 to 0.0625
- up_proj: bfloat16 [4, 4, 7168, 2048], P('row', 'col'), may hold values from -0.0625 to 0.0625
- down_proj: bfloat16 [4, 4, 2048, 7168], P('row', 'col'), may hold values from -0.125 to 0.125
Outputs:
- layer_out: bfloat16 [128, 7168], P(('groups', 'row', 'col')), parts along dimension 0
The draws below stay inside these ranges and needn't reach their ends.
There are 2 independent parts, one for each index of `groups`. The reference program is written for one: setup_inputs(seed, part) draws one part's arguments, and reference() takes and returns one part's arrays. A program takes and returns all parts, laid end to end along the dimension named above; an argument that names none is the same for every part. Nothing has to cross between parts.
Inputs may be any that keep to these rules, and one draw needn't show every extreme that they name: `expert_ids`: each row names 8 different experts; within the rows of one device (aligned blocks of 4 rows) no expert is named by more than 3 rows, and in some such block some expert is named by exactly 3 rows.
All inputs are finite; a program needn't handle non-finite values.
Results may differ from the reference program's by a relative error of at most 0.0085.
Values may be sent and summed in bfloat16 or wider, within the bound.
No kernel may reach another device: no remote copies, remote signals or barrier semaphores. Data moves between devices by JAX's collectives and lax.ppermute only.
A program may use at most 192 MiB of HBM per device.

```python
import math
import jax
import jax.numpy as jnp
import numpy as np
from jax import lax

D = 7168
FF = 2048
TOP = 8
TOK_DEV = 4
SLICES = 1
FF_DEV = 2048
EXPERTS = 16
SLOTS = 3
TOKENS = 64
N_ROW = 4
N_COL = 4


def levels(own_key, extent, split, low, top_value):
    def one(axis_at, parts):
        steps = jax.random.uniform(jax.random.fold_in(jax.random.fold_in(own_key, 6), axis_at), (parts,), jnp.float32, low / len(split), top_value / len(split))
        return jnp.repeat(jnp.exp(steps), extent[axis_at] // parts).reshape((-1,) + (1,) * (len(extent) - axis_at - 1))

    factor_of = one(*split[0])
    for cut in split[1:]:
        factor_of = factor_of * one(*cut)
    return factor_of


def deal_out(own_key, own, number, rows, amount, top, most, slope):
    order = jax.random.permutation(own_key, amount)
    packed, ordinary = load_shares(amount, rows * top, most, slope, True), load_shares(amount, rows * top, most, slope, False)
    places = jnp.arange(amount)

    def named(sizes, offset_by):
        used = int((sizes > 0).sum())
        fixed = max(1, used // 4)
        shifted = fixed + (places - fixed + offset_by * (used - fixed)) % max(1, amount - fixed)
        return jnp.zeros((amount,), jnp.int32).at[order[jnp.where(places < fixed, places, shifted)]].set(jnp.asarray(sizes, jnp.int32))

    sizes = jnp.where(number % 4 == 0, named(packed, number // 4), named(ordinary, number - number // 4 - 1))
    mixed = jax.random.permutation(jax.random.fold_in(own, 3), amount)
    source_of, taker = mixed[0:amount // 2 * 2:2], mixed[1:amount // 2 * 2:2]
    slack = jnp.minimum(sizes[source_of] - 1, most - sizes[taker]) // 2
    slack = jnp.where((source_of == order[0]) | (taker == order[0]) | (sizes[taker] == 0), 0, jnp.maximum(slack, 0))
    shifted = jax.random.randint(jax.random.fold_in(own, 4), (amount // 2,), 0, 1 << 20) % (slack + 1)
    sizes = sizes.at[source_of].add(-shifted).at[taker].add(shifted)
    items = jnp.searchsorted(jnp.cumsum(sizes), jnp.arange(rows * top), side="right").astype(jnp.int32)
    table = items.reshape(top, rows).T
    table = table[jax.random.permutation(jax.random.fold_in(own, 1), rows)]
    offset_by = jax.random.randint(jax.random.fold_in(own, 2), (rows, 1), 0, top)
    return jnp.take_along_axis(table, (jnp.arange(top)[None, :] + offset_by) % top, axis=1)


def load_shares(amount, total, limit, slope, full):
    weights = [(1 << 20) // math.isqrt(grade ** slope) + 1 for grade in range(1, amount + 1)]
    largest = limit if full else min(limit, max(-(-total // amount), total * weights[0] // sum(weights)))
    least = 1 if total - largest >= amount - 1 else 0
    holding, surplus = [largest] + [least] * (amount - 1), total - largest - least * (amount - 1)
    while surplus > 0:
        candidates = [i for i in range(1, amount) if holding[i] < largest] or [i for i in range(1, amount) if holding[i] < limit]
        whole, left = sum([weights[i] for i in candidates]), surplus
        for i in candidates:
            more = min(limit - holding[i], max(1, left * weights[i] // whole), surplus)
            holding[i] = holding[i] + more
            surplus = surplus - more
    return np.array(holding)


def gaussian(key, extent, width, limit, cuts=(), kind=jnp.bfloat16):
    drawn = jax.random.normal(key, extent, jnp.float32) * width
    if len(cuts) > 0:
        drawn = levels(key, extent, cuts, -0.22, 0.18) * drawn
    return jnp.clip(drawn, min=-limit, max=limit).astype(kind)


def setup_inputs(seed: int = 0, part: int = 0) -> dict:
    key_of = jax.random.split(jax.random.key(seed), 8)
    part_keys = jax.random.split(jax.random.fold_in(key_of[7], part), 8)
    tokens = gaussian(part_keys[0], (TOKENS, D), 1.0, 6.0, ((0, 16),))
    expert_ids_keys = jax.random.split(jax.random.fold_in(part_keys[1], 1), TOKENS // TOK_DEV)
    expert_ids_turns = jax.random.permutation(jax.random.fold_in(part_keys[1], 3), TOKENS // TOK_DEV)
    expert_ids = jax.vmap(lambda own, number: deal_out(jax.random.fold_in(part_keys[1], 2), own, number, TOK_DEV, EXPERTS, TOP, SLOTS, 2))(expert_ids_keys, expert_ids_turns).reshape((TOKENS, TOP))
    route_weight = jnp.clip(0.099609375 + 0.49804688 * jax.random.uniform(part_keys[2], (TOKENS, TOP), jnp.float32) ** levels(part_keys[2], (TOKENS, TOP), ((0, 16),), -0.2, 0.2), 0.099609375, 0.59765625).astype(jnp.bfloat16)
    dither = jnp.clip(1.0 * jax.random.uniform(part_keys[3], (TOKENS, N_ROW, D), jnp.float32) ** levels(part_keys[3], (TOKENS, N_ROW, D), ((0, 16),), -0.2, 0.2), 0.0, 1.0).astype(jnp.bfloat16)
    gate_proj = gaussian(key_of[4], (N_ROW, N_COL, D, FF_DEV), D ** -0.5, 0.0625, ((0, 4), (1, 4)))
    up_proj = gaussian(key_of[5], (N_ROW, N_COL, D, FF_DEV), D ** -0.5, 0.0625, ((0, 4), (1, 4)))
    down_proj = gaussian(key_of[6], (N_ROW, N_COL, FF_DEV, D), FF ** -0.5, 0.125, ((0, 4), (1, 4)))
    return dict(tokens=tokens, expert_ids=expert_ids, route_weight=route_weight, dither=dither, gate_proj=gate_proj, up_proj=up_proj, down_proj=down_proj)


def reference(tokens, expert_ids, route_weight, dither, gate_proj, up_proj, down_proj):
    row_experts = N_COL // SLICES
    capacity = min(TOKENS, N_ROW * N_COL * SLOTS)
    positions = jnp.arange(TOKENS, dtype=jnp.int32)
    weights_f = route_weight.astype(jnp.float32)

    def per_expert(carry, expert):
        matches = expert_ids == expert
        factors = jnp.sum(jnp.where(matches, weights_f, 0.0), axis=1)
        picked = jnp.any(matches, axis=1)
        sort_keys = jnp.where(picked, positions, positions + TOKENS)
        chosen = jnp.argsort(sort_keys)[:capacity].astype(jnp.int32)
        inputs = tokens[chosen].astype(jnp.float32)
        grid_row = (expert // row_experts).astype(jnp.int32)
        grid_col = ((expert % row_experts) * SLICES).astype(jnp.int32)
        gate_slab = lax.dynamic_slice_in_dim(lax.dynamic_index_in_dim(gate_proj, grid_row, 0, keepdims=False), grid_col, SLICES, 0)
        up_slab = lax.dynamic_slice_in_dim(lax.dynamic_index_in_dim(up_proj, grid_row, 0, keepdims=False), grid_col, SLICES, 0)
        down_slab = lax.dynamic_slice_in_dim(lax.dynamic_index_in_dim(down_proj, grid_row, 0, keepdims=False), grid_col, SLICES, 0)
        gate_pre = jnp.einsum("cd,sdf->csf", inputs, gate_slab.astype(jnp.float32))
        up_pre = jnp.einsum("cd,sdf->csf", inputs, up_slab.astype(jnp.float32))
        hidden = (jax.nn.silu(gate_pre) * up_pre).astype(jnp.bfloat16)
        partial_value = jnp.einsum("csf,sfd->csd", hidden.astype(jnp.float32), down_slab.astype(jnp.float32)).astype(jnp.bfloat16)
        expert_out = jnp.sum(partial_value.astype(jnp.float32), axis=1)
        contrib = factors[chosen][:, None] * expert_out
        carry = carry.at[chosen, grid_row].add(contrib)
        return carry, None

    combined = jnp.zeros((TOKENS, N_ROW, D), jnp.float32)
    combined, _ = lax.scan(per_expert, combined, jnp.arange(EXPERTS, dtype=jnp.int32))
    spread = 0.125 * jnp.max(jnp.abs(combined), axis=2, keepdims=True)
    dithered = (combined + spread * (dither.astype(jnp.float32) - 0.5)).astype(jnp.bfloat16)
    return jnp.sum(dithered.astype(jnp.float32), axis=1).astype(jnp.bfloat16)
```

```python
import functools

import jax
import jax.numpy as jnp
from jax import lax
from jax.experimental import pallas as pl
from jax.experimental.pallas import tpu as pltpu
from jax.sharding import PartitionSpec as P

FF = 2048
LANES = 128
COLS = 256
MIB = 2**20
VMEM = pl.BlockSpec(memory_space=pltpu.VMEM)
HBM = pl.BlockSpec(memory_space=pltpu.HBM)


def params(mib):
    return pltpu.CompilerParams(vmem_limit_bytes=int(mib * MIB))


def cost(flops, moved):
    return pl.CostEstimate(flops=flops, bytes_accessed=moved, transcendentals=0)


def flip(count, bit):
    return [(i, i ^ bit) for i in range(count)]


def expert_apply(batch, gate_local, up_local, down_local):
    flat = batch.reshape(-1, batch.shape[-1])
    gate_pre = jnp.dot(flat, gate_local, preferred_element_type=jnp.float32)
    up_pre = jnp.dot(flat, up_local, preferred_element_type=jnp.float32)
    hidden = (jax.nn.silu(gate_pre) * up_pre).astype(jnp.bfloat16)
    partial_value = jnp.dot(hidden, down_local, preferred_element_type=jnp.float32).astype(
        jnp.bfloat16
    )
    return partial_value.reshape(batch.shape)


def local_any(tokens, expert_ids, route_weight, dither, gate_proj, up_proj, down_proj):
    row_count = lax.axis_size("row")
    col_count = lax.axis_size("col")
    tok_count = tokens.shape[0]
    model_width = tokens.shape[1]
    pieces = FF // gate_proj.shape[3]
    per_row = col_count // pieces
    slot_count = 3 * tok_count // 4
    expert_count = row_count * per_row
    labels = lax.broadcasted_iota(jnp.int32, (1, 1, expert_count), 2)
    matches = expert_ids[:, :, None] == labels
    counted = jnp.sum(matches.astype(jnp.int32), axis=1)
    weighted = jnp.sum(
        jnp.where(matches, route_weight[:, :, None].astype(jnp.float32), 0.0), axis=1
    )
    before = jnp.cumsum(counted, axis=0) - counted
    slot_ids = lax.broadcasted_iota(jnp.int32, (1, 1, slot_count), 2)
    placed = (counted[:, :, None] == 1) & (before[:, :, None] == slot_ids)
    placed = placed.reshape(tok_count, row_count, per_row, slot_count)
    shares = (
        placed.astype(jnp.float32) * weighted.reshape(tok_count, row_count, per_row)[:, :, :, None]
    )
    place_bf = placed.astype(jnp.bfloat16)
    outgoing = jnp.einsum(
        "trjm,td->jrmd", place_bf, tokens, preferred_element_type=jnp.float32
    ).astype(jnp.bfloat16)
    share_out = jnp.transpose(shares, (2, 1, 3, 0)).astype(jnp.bfloat16)
    arrived, arrived_share, arrived_dither = (
        lax.all_to_all(outgoing, "row", split_axis=1, concat_axis=1, tiled=True),
        lax.all_to_all(share_out, "row", split_axis=1, concat_axis=1, tiled=True),
        lax.all_to_all(dither, "row", split_axis=1, concat_axis=1, tiled=True),
    )
    fanned = jnp.broadcast_to(arrived[:, None], (per_row, pieces) + arrived.shape[1:])
    fanned = fanned.reshape((col_count,) + arrived.shape[1:])
    returned = lax.all_to_all(
        expert_apply(
            lax.all_to_all(fanned, "col", split_axis=0, concat_axis=0, tiled=True),
            gate_proj[0, 0],
            up_proj[0, 0],
            down_proj[0, 0],
        ),
        "col",
        split_axis=0,
        concat_axis=0,
        tiled=True,
    )
    merged = jnp.sum(
        returned.reshape(per_row, pieces, row_count, slot_count, model_width).astype(jnp.float32),
        axis=1,
    )
    combined = jnp.einsum(
        "jrmt,jrmd->trd", arrived_share.astype(jnp.float32), merged, precision=lax.Precision.HIGHEST
    )
    spread = 0.125 * jnp.max(jnp.abs(combined), axis=2, keepdims=True)
    rounded = (combined + spread * (arrived_dither.astype(jnp.float32) - 0.5)).astype(jnp.bfloat16)
    collected = lax.all_to_all(rounded, "row", split_axis=1, concat_axis=1, tiled=True)
    return jnp.sum(collected.astype(jnp.float32), axis=1).astype(jnp.bfloat16)


N = 4
SLOTS = 3
BLOCKS = N * N
ROWS = BLOCKS * 4
HELD = 14
PACKED = N * SLOTS * N


def pack_kernel(tok_ref, ids_ref, share_ref, out_ref):
    width = tok_ref.shape[1]
    out_ref[:, :width] = tok_ref[...]
    tail = jnp.concatenate(
        [
            ids_ref[...].astype(jnp.float32),
            share_ref[...].astype(jnp.float32),
            jnp.zeros((4, LANES - 16), jnp.float32),
        ],
        axis=1,
    )
    out_ref[:, width:] = tail.astype(jnp.bfloat16)


def stack_kernel(*refs):
    out_ref = refs[-1]
    parts = [r[...].astype(jnp.float32) for r in refs[:-1]]
    out_ref[...] = jnp.concatenate(parts, axis=0).astype(jnp.bfloat16)


def fill_kernel(first, last, fresh, *refs):
    gate_ref, up_ref = refs[0], refs[1]
    buf, sem = refs[-2], refs[-1]
    copies = [block_copy(gate_ref, up_ref, buf, sem, i) for i in range(first, last)]
    for c in copies:
        c.start()
    for c in copies:
        c.wait()


def block_copy(gate_ref, up_ref, buf, sem, i):
    src = (gate_ref, up_ref)[i % 2]
    return pltpu.make_async_copy(
        src.at[:, pl.ds((i // 2) * COLS, COLS)], buf.at[i % HELD], sem.at[i]
    )


def down_copy(down_ref, buf, sem, b):
    deep = down_ref.shape[0]
    return pltpu.make_async_copy(
        down_ref.at[:, pl.ds(b * COLS, COLS)],
        buf.at[2 + b // 3, pl.ds((b % 3) * deep, deep)],
        sem.at[b],
    )


def down_block(buf, deep, b):
    return buf[2 + b // 3, (b % 3) * deep : (b % 3 + 1) * deep, :]


def routing(meta, me_row, me_col):
    ids, share = meta[:, :8], meta[:, 8:16]
    at = lax.broadcasted_iota(jnp.int32, (ROWS, ROWS), 0)
    to = lax.broadcasted_iota(jnp.int32, (ROWS, ROWS), 1)
    earlier = ((at // 4 == to // 4) & (to < at)).astype(jnp.bfloat16)
    found, rank, weight = [], [], []
    for k in range(N):
        expert = (me_row * N + (me_col ^ k)).astype(jnp.float32)
        hit = (ids == expert).astype(jnp.float32)
        found.append(jnp.sum(hit, axis=1, keepdims=True))
        weight.append(jnp.sum(hit * share, axis=1, keepdims=True))
    lanes = jnp.concatenate(found + [jnp.zeros((ROWS, LANES - N), jnp.float32)], axis=1)
    rank = jnp.dot(earlier, lanes.astype(jnp.bfloat16), preferred_element_type=jnp.float32)
    return found, rank, weight


def store_outs(value, outs, lo):
    width = value.shape[1]
    for k in range(N):
        for s in range(SLOTS):
            at = (k * SLOTS + s) * N
            outs[k][s, :, lo : lo + width] = value[at : at + N].astype(jnp.bfloat16)


def hidden_kernel(ready, blocks, *refs):
    pieces = refs[:4]
    gate_ref, up_ref, down_ref, _ = refs[4:8]
    outs, hid_ref, mix_ref, buf = refs[8:12], refs[12], refs[13], refs[14]
    x_ref, h_ref, fill_sem, down_sem = refs[15:]
    width = x_ref.shape[1]
    deep = down_ref.shape[0]
    for i in range(ready, HELD):
        block_copy(gate_ref, up_ref, buf, fill_sem, i).start()
    for q in range(4):
        x_ref[q * 16 : (q + 1) * 16, :] = pieces[q][:, :width]

    def product(j):
        at = lax.rem(2 * j, HELD)
        g = jnp.dot(x_ref[...], buf[at], preferred_element_type=jnp.float32)
        u = jnp.dot(x_ref[...], buf[at + 1], preferred_element_type=jnp.float32)
        h_ref[:, pl.ds(pl.multiple_of(j * COLS, COLS), COLS)] = (
            g / (1.0 + jnp.exp(-g)) * u
        ).astype(jnp.bfloat16)

    def step(j, carry):
        for half in range(2):
            i = 2 * j + half

            @pl.when(i >= ready)
            def _():
                src = (gate_ref, up_ref)[half]
                pltpu.make_async_copy(
                    src.at[:, pl.ds(pl.multiple_of(j * COLS, COLS), COLS)],
                    buf.at[lax.rem(i, HELD)],
                    fill_sem.at[i],
                ).wait()

        product(j)

        @pl.when(j == 0)
        def _():
            for i in range(HELD, 16):
                block_copy(gate_ref, up_ref, buf, fill_sem, i).start()

        for n in range(6):
            b = 6 * (j - 1) + n

            @pl.when((b >= 0) & (b < width // COLS))
            def _():
                pltpu.make_async_copy(
                    down_ref.at[:, pl.ds(pl.multiple_of(b * COLS, COLS), COLS)],
                    buf.at[2 * j + n // 3, pl.ds((n % 3) * deep, deep)],
                    down_sem.at[b],
                ).start()

        return carry

    lax.fori_loop(0, 8, step, 0)

    meta = jnp.concatenate(
        [pieces[q][:, width:].astype(jnp.float32) for q in range(4)], axis=0
    )
    found, rank, weight = routing(meta, lax.axis_index("row"), lax.axis_index("col"))
    m_at = lax.broadcasted_iota(jnp.int32, (ROWS, PACKED), 0)
    c_at = lax.broadcasted_iota(jnp.int32, (ROWS, PACKED), 1)
    same = (m_at // 16 == c_at % 4) & ((m_at // 4) % 4 == c_at // 12)
    slot = ((c_at // 4) % 3).astype(jnp.float32)
    take = jnp.where(same & (found[0] > 0) & (rank[:, 0:1] == slot), 1.0, 0.0)
    hid = lax.dot_general(
        take.astype(jnp.bfloat16),
        h_ref[...],
        (((0,), (0,)), ((), ())),
        preferred_element_type=jnp.float32,
    )
    hid_ref[...] = hid.astype(jnp.bfloat16)
    mix = jnp.zeros((ROWS, PACKED), jnp.float32)
    for k in range(N):
        here = (c_at // 12 == k) & (m_at // 16 == c_at % 4)
        mix = jnp.where(here & (found[k] > 0) & (rank[:, k : k + 1] == slot), weight[k], mix)
    for q in range(N):
        mix_ref[q * 4 : q * 4 + 4, :] = mix[q * 16 : q * 16 + 4]
    for b in range(width // COLS):
        down_copy(down_ref, buf, down_sem, b).wait()
    for b in range(blocks):
        value = jnp.dot(hid_ref[...], down_block(buf, deep, b), preferred_element_type=jnp.float32)
        store_outs(value, outs, b * COLS)


def down_kernel(first, last, deep, hid_ref, buf, *outs):
    for b in range(first, last):
        value = jnp.dot(hid_ref[...], down_block(buf, deep, b), preferred_element_type=jnp.float32)
        store_outs(value, outs, (b - first) * COLS)


def merge_kernel(mix_ref, *refs):
    ins, outs = refs[:4], refs[4:]
    got = jnp.concatenate(
        [ins[k][s].astype(jnp.float32) for k in range(N) for s in range(SLOTS)], axis=0
    ).astype(jnp.bfloat16)
    value = jnp.dot(
        mix_ref[...].astype(jnp.bfloat16), got, preferred_element_type=jnp.float32
    )
    for q in range(N):
        outs[q][...] = value[q * 4 : q * 4 + 4].astype(jnp.bfloat16)


def draw_kernel(dither_ref, out_ref):
    draw = dither_ref[...].astype(jnp.float32)
    at = lax.broadcasted_iota(jnp.int32, draw.shape, 1)
    for q in range(N):
        mine = jnp.where(at == (lax.axis_index("row") ^ q), draw, 0.0)
        out_ref[q] = (jnp.sum(mine, axis=1) - 0.5).astype(out_ref.dtype)


def final_kernel(chunks, draw_ref, *refs):
    ins, out_ref = refs[:-1], refs[-1]
    total = None
    for q in range(N):
        part = jnp.concatenate(
            [ins[c * N + q][...].astype(jnp.float32) for c in range(chunks)], axis=1
        )
        spread = 0.125 * jnp.max(jnp.abs(part), axis=1, keepdims=True)
        part = part + spread * draw_ref[q]
        total = part if total is None else total + part
    out_ref[...] = total.astype(jnp.bfloat16)


def local_grid(tokens, expert_ids, route_weight, dither, gate_proj, up_proj, down_proj):
    gate, up, down = gate_proj[0, 0], up_proj[0, 0], down_proj[0, 0]
    width, wide = gate.shape
    deep = down.shape[0]
    bf = jnp.bfloat16
    shape = jax.ShapeDtypeStruct
    anyw = pl.BlockSpec(memory_space=pl.ANY)
    pin = lambda a: pltpu.with_memory_space_constraint(a, pltpu.VMEM)

    packed = pl.pallas_call(
        pack_kernel,
        out_shape=shape((4, width + LANES), bf),
        in_specs=[VMEM] * 3,
        out_specs=VMEM,
        compiler_params=params(6),
        name="pack",
    )(tokens, expert_ids, route_weight)
    near = [packed] + [lax.ppermute(packed, "col", flip(N, k)) for k in (1, 2, 3)]

    buf_type = pltpu.VMEM((HELD, width, COLS), bf)
    block_bytes = width * COLS * 2
    split = (6, 13)
    buf = pl.pallas_call(
        functools.partial(fill_kernel, 0, split[0], True),
        out_shape=buf_type,
        in_specs=[HBM] * 2 + [anyw],
        out_specs=VMEM,
        scratch_shapes=[pltpu.SemaphoreType.DMA((16,))],
        compiler_params=params(6),
        cost_estimate=cost(0, split[0] * block_bytes),
        name="fill_a",
    )(gate, up, packed)
    *near, buf = lax.optimization_barrier((*near, buf))
    own = pl.pallas_call(
        stack_kernel,
        out_shape=shape((16, width + LANES), bf),
        in_specs=[VMEM] * 4,
        out_specs=VMEM,
        compiler_params=params(6),
        name="stack",
    )(*near)
    by_core = lax.ppermute(own, "row", flip(N, 1))
    by_x = lax.ppermute(own, "row", flip(N, 2))
    buf = pl.pallas_call(
        functools.partial(fill_kernel, split[0], split[1], False),
        out_shape=buf_type,
        in_specs=[HBM] * 2 + [VMEM, anyw],
        out_specs=VMEM,
        scratch_shapes=[pltpu.SemaphoreType.DMA((16,))],
        input_output_aliases={2: 0},
        compiler_params=params(6),
        cost_estimate=cost(0, (split[1] - split[0]) * block_bytes),
        name="fill_b",
    )(gate, up, pin(buf), own)
    by_x, buf = lax.optimization_barrier((by_x, buf))
    by_both = lax.ppermute(by_x, "row", flip(N, 1))

    chunks = (14, 14)
    outs = [shape((SLOTS, N, n * COLS), bf) for n in chunks]
    first = pl.pallas_call(
        functools.partial(hidden_kernel, split[1], chunks[0]),
        out_shape=[outs[0]] * 4
        + [shape((PACKED, wide), bf), shape((16, PACKED), jnp.float32), buf_type],
        in_specs=[VMEM] * 4 + [HBM] * 3 + [VMEM],
        out_specs=[VMEM] * 7,
        scratch_shapes=[
            pltpu.VMEM((ROWS, width), bf),
            pltpu.VMEM((ROWS, wide), bf),
            pltpu.SemaphoreType.DMA((16,)),
            pltpu.SemaphoreType.DMA((width // COLS,)),
        ],
        input_output_aliases={7: 6},
        compiler_params=params(6),
        cost_estimate=cost(2 * ROWS * width * wide * 3, 40 * MIB),
        name="hidden",
    )(own, by_core, by_x, by_both, gate, up, down, pin(buf))
    hid, mix, buf = first[4:]
    parts = [first[:4]]
    parts.append(
        pl.pallas_call(
            functools.partial(down_kernel, chunks[0], chunks[0] + chunks[1], deep),
            out_shape=[outs[1]] * 4,
            in_specs=[VMEM, VMEM],
            out_specs=[VMEM] * 4,
            compiler_params=params(6),
            cost_estimate=cost(2 * ROWS * width * wide, 10 * MIB),
            name="down",
        )(hid, pin(buf))
    )
    draws = pl.pallas_call(
        draw_kernel,
        out_shape=shape((N, 4, width), jnp.float32),
        in_specs=[VMEM],
        out_specs=VMEM,
        compiler_params=params(6),
        name="draws",
    )(dither)
    finals = []
    for c, part in enumerate(parts):
        got = [part[0]] + [lax.ppermute(part[k], "col", flip(N, k)) for k in (1, 2, 3)]
        value = pl.pallas_call(
            merge_kernel,
            out_shape=[shape((4, chunks[c] * COLS), bf)] * 4,
            in_specs=[VMEM] * 5,
            out_specs=[VMEM] * 4,
            compiler_params=params(6),
            name="merge",
        )(mix, *got)
        finals += [value[0]] + [lax.ppermute(value[q], "row", flip(N, q)) for q in (1, 2, 3)]
    return pl.pallas_call(
        functools.partial(final_kernel, len(chunks)),
        out_shape=shape((4, width), bf),
        in_specs=[VMEM] * (1 + len(finals)),
        out_specs=VMEM,
        compiler_params=params(6),
        name="final",
    )(draws, *finals)


def solution(mesh):
    def local(tokens, expert_ids, route_weight, dither, gate_proj, up_proj, down_proj):
        grid = (mesh.shape["row"], mesh.shape["col"]) == (N, N)
        whole_expert = gate_proj.shape[3] == FF and tokens.shape[0] == 4
        pick = local_grid if grid and whole_expert else local_any
        return pick(tokens, expert_ids, route_weight, dither, gate_proj, up_proj, down_proj)

    return jax.shard_map(
        local,
        mesh=mesh,
        in_specs=(
            P(("groups", "row", "col"), None),
            P(("groups", "row", "col"), None),
            P(("groups", "row", "col"), None),
            P(("groups", "row", "col"), None, None),
            P("row", "col", None, None),
            P("row", "col", None, None),
            P("row", "col", None, None),
        ),
        out_specs=P(("groups", "row", "col"), None),
        check_vma=False,
    )
```

```python
import functools

import jax
import jax.numpy as jnp
from jax import lax
from jax.experimental import pallas as pl
from jax.experimental.pallas import tpu as pltpu
from jax.sharding import PartitionSpec as P

FF = 2048
LANES = 128
COLS = 256
PAIR = 2 * COLS
MIB = 2**20
VMEM = pl.BlockSpec(memory_space=pltpu.VMEM)
HBM = pl.BlockSpec(memory_space=pltpu.HBM)


def params(mib):
    return pltpu.CompilerParams(vmem_limit_bytes=int(mib * MIB))


def cost(flops, moved):
    return pl.CostEstimate(flops=flops, bytes_accessed=moved, transcendentals=0)


def flip(count, bit):
    return [(i, i ^ bit) for i in range(count)]


def expert_apply(batch, gate_local, up_local, down_local):
    flat = batch.reshape(-1, batch.shape[-1])
    gate_pre = jnp.dot(flat, gate_local, preferred_element_type=jnp.float32)
    up_pre = jnp.dot(flat, up_local, preferred_element_type=jnp.float32)
    hidden = (jax.nn.silu(gate_pre) * up_pre).astype(jnp.bfloat16)
    partial_value = jnp.dot(hidden, down_local, preferred_element_type=jnp.float32).astype(
        jnp.bfloat16
    )
    return partial_value.reshape(batch.shape)


def local_any(tokens, expert_ids, route_weight, dither, gate_proj, up_proj, down_proj):
    row_count = lax.axis_size("row")
    col_count = lax.axis_size("col")
    tok_count = tokens.shape[0]
    model_width = tokens.shape[1]
    pieces = FF // gate_proj.shape[3]
    per_row = col_count // pieces
    slot_count = 3 * tok_count // 4
    expert_count = row_count * per_row
    labels = lax.broadcasted_iota(jnp.int32, (1, 1, expert_count), 2)
    matches = expert_ids[:, :, None] == labels
    counted = jnp.sum(matches.astype(jnp.int32), axis=1)
    weighted = jnp.sum(
        jnp.where(matches, route_weight[:, :, None].astype(jnp.float32), 0.0), axis=1
    )
    before = jnp.cumsum(counted, axis=0) - counted
    slot_ids = lax.broadcasted_iota(jnp.int32, (1, 1, slot_count), 2)
    placed = (counted[:, :, None] == 1) & (before[:, :, None] == slot_ids)
    placed = placed.reshape(tok_count, row_count, per_row, slot_count)
    shares = (
        placed.astype(jnp.float32) * weighted.reshape(tok_count, row_count, per_row)[:, :, :, None]
    )
    place_bf = placed.astype(jnp.bfloat16)
    outgoing = jnp.einsum(
        "trjm,td->jrmd", place_bf, tokens, preferred_element_type=jnp.float32
    ).astype(jnp.bfloat16)
    share_out = jnp.transpose(shares, (2, 1, 3, 0)).astype(jnp.bfloat16)
    arrived, arrived_share, arrived_dither = (
        lax.all_to_all(outgoing, "row", split_axis=1, concat_axis=1, tiled=True),
        lax.all_to_all(share_out, "row", split_axis=1, concat_axis=1, tiled=True),
        lax.all_to_all(dither, "row", split_axis=1, concat_axis=1, tiled=True),
    )
    fanned = jnp.broadcast_to(arrived[:, None], (per_row, pieces) + arrived.shape[1:])
    fanned = fanned.reshape((col_count,) + arrived.shape[1:])
    returned = lax.all_to_all(
        expert_apply(
            lax.all_to_all(fanned, "col", split_axis=0, concat_axis=0, tiled=True),
            gate_proj[0, 0],
            up_proj[0, 0],
            down_proj[0, 0],
        ),
        "col",
        split_axis=0,
        concat_axis=0,
        tiled=True,
    )
    merged = jnp.sum(
        returned.reshape(per_row, pieces, row_count, slot_count, model_width).astype(jnp.float32),
        axis=1,
    )
    combined = jnp.einsum(
        "jrmt,jrmd->trd", arrived_share.astype(jnp.float32), merged, precision=lax.Precision.HIGHEST
    )
    spread = 0.125 * jnp.max(jnp.abs(combined), axis=2, keepdims=True)
    rounded = (combined + spread * (arrived_dither.astype(jnp.float32) - 0.5)).astype(jnp.bfloat16)
    collected = lax.all_to_all(rounded, "row", split_axis=1, concat_axis=1, tiled=True)
    return jnp.sum(collected.astype(jnp.float32), axis=1).astype(jnp.bfloat16)


N = 4
SLOTS = 3
BLOCKS = N * N
ROWS = BLOCKS * 4
HELD = 3
PACKED = N * SLOTS * N


def pack_kernel(tok_ref, ids_ref, share_ref, _, out_ref, ids_here, share_here, sem):
    width = tok_ref.shape[1]
    copies = [
        pltpu.make_async_copy(ids_ref, ids_here, sem.at[0]),
        pltpu.make_async_copy(share_ref, share_here, sem.at[1]),
        pltpu.make_async_copy(tok_ref, out_ref.at[:, pl.ds(0, width)], sem.at[2]),
    ]
    for c in copies:
        c.start()
    for c in copies:
        c.wait()
    tail = jnp.concatenate(
        [
            ids_here[...].astype(jnp.float32),
            share_here[...].astype(jnp.float32),
            jnp.zeros((4, LANES - 16), jnp.float32),
        ],
        axis=1,
    )
    out_ref[:, width:] = tail.astype(jnp.bfloat16)


def stack_kernel(*refs):
    out_ref = refs[-1]
    parts = [r[...].astype(jnp.float32) for r in refs[:4]]
    out_ref[...] = jnp.concatenate(parts, axis=0).astype(jnp.bfloat16)


def up_copy(up_ref, buf, sem, j):
    return pltpu.make_async_copy(
        up_ref.at[:, pl.ds(j * PAIR, PAIR)], buf.at[j % HELD], sem.at[j]
    )


def routing(meta, me_row, me_col):
    ids, share = meta[:, :8], meta[:, 8:16]
    at = lax.broadcasted_iota(jnp.int32, (ROWS, ROWS), 0)
    to = lax.broadcasted_iota(jnp.int32, (ROWS, ROWS), 1)
    earlier = ((at // 4 == to // 4) & (to < at)).astype(jnp.bfloat16)
    found, rank, weight = [], [], []
    for k in range(N):
        expert = (me_row * N + (me_col ^ k)).astype(jnp.float32)
        hit = (ids == expert).astype(jnp.float32)
        found.append(jnp.sum(hit, axis=1, keepdims=True))
        weight.append(jnp.sum(hit * share, axis=1, keepdims=True))
    lanes = jnp.concatenate(found + [jnp.zeros((ROWS, LANES - N), jnp.float32)], axis=1)
    rank = jnp.dot(earlier, lanes.astype(jnp.bfloat16), preferred_element_type=jnp.float32)
    return found, rank, weight


def store_outs(value, outs, lo):
    width = value.shape[1]
    for k in range(N):
        for s in range(SLOTS):
            at = (k * SLOTS + s) * N
            outs[k][s, :, lo : lo + width] = value[at : at + N].astype(jnp.bfloat16)


def hidden_kernel(blocks, *refs):
    pieces = refs[:4]
    gate_ref, up_ref, down_ref = refs[4:7]
    outs, hid_ref, mix_ref = refs[7:11], refs[11], refs[12]
    x_ref, h_ref, buf, piece_sem, fill_sem, down_sem = refs[13:]
    width = gate_ref.shape[0]
    deep = down_ref.shape[0]
    steps = deep // PAIR
    bring = [
        pltpu.make_async_copy(pieces[q], x_ref.at[pl.ds(q * 16, 16)], piece_sem.at[q])
        for q in range(N)
    ]
    for c in bring:
        c.start()
    for j in range(HELD):
        up_copy(up_ref, buf, fill_sem, j).start()
    x_ref[ROWS:, :] = jnp.zeros((x_ref.shape[0] - ROWS, x_ref.shape[1]), x_ref.dtype)
    for c in bring:
        c.wait()

    def down_place(b):
        return buf.at[(1 + b // 3) % HELD, pl.ds(b % 3 * deep, deep)]

    def down_copy(b):
        return pltpu.make_async_copy(
            down_ref.at[:, pl.ds(b * PAIR, PAIR)], down_place(b), down_sem.at[b]
        )

    for j in range(steps):
        at = pl.ds(j * PAIR, PAIR)
        g = jnp.dot(x_ref[:, :width], gate_ref[:, at], preferred_element_type=jnp.float32)[:ROWS]
        up_copy(up_ref, buf, fill_sem, j).wait()
        u = jnp.dot(x_ref[:, :width], buf[j % HELD], preferred_element_type=jnp.float32)[:ROWS]
        h_ref[:, at] = (g / (1.0 + jnp.exp(-g)) * u).astype(jnp.bfloat16)
        if j + HELD < steps:
            up_copy(up_ref, buf, fill_sem, j + HELD).start()
        if j > 0:
            for b in range(3 * (j - 1), min(3 * j, blocks)):
                down_copy(b).start()

    meta = x_ref[:ROWS, width:].astype(jnp.float32)
    found, rank, weight = routing(meta, lax.axis_index("row"), lax.axis_index("col"))
    m_at = lax.broadcasted_iota(jnp.int32, (ROWS, PACKED), 0)
    c_at = lax.broadcasted_iota(jnp.int32, (ROWS, PACKED), 1)
    same = (m_at // 16 == c_at % 4) & ((m_at // 4) % 4 == c_at // 12)
    slot = ((c_at // 4) % 3).astype(jnp.float32)
    take = jnp.where(same & (found[0] > 0) & (rank[:, 0:1] == slot), 1.0, 0.0)
    hid = lax.dot_general(
        take.astype(jnp.bfloat16),
        h_ref[...],
        (((0,), (0,)), ((), ())),
        preferred_element_type=jnp.float32,
    )
    hid_ref[...] = hid.astype(jnp.bfloat16)
    mix = jnp.zeros((ROWS, PACKED), jnp.float32)
    for k in range(N):
        here = (c_at // 12 == k) & (m_at // 16 == c_at % 4)
        mix = jnp.where(here & (found[k] > 0) & (rank[:, k : k + 1] == slot), weight[k], mix)
    for q in range(N):
        mix_ref[q * 4 : q * 4 + 4, :] = mix[q * 16 : q * 16 + 4]
    for b in range(blocks):
        down_copy(b).wait()
        value = jnp.dot(
            hid_ref[...],
            down_place(b)[...],
            preferred_element_type=jnp.float32,
        )
        store_outs(value, outs, b * PAIR)


def down_kernel(first, last, hid_from, down_ref, *refs):
    outs, buf, hid_ref, sem, hid_sem = refs[:4], refs[4], refs[5], refs[6], refs[7]
    bring = pltpu.make_async_copy(hid_from, hid_ref, hid_sem)
    bring.start()
    copies = [
        pltpu.make_async_copy(down_ref.at[:, pl.ds(b * PAIR, PAIR)], buf.at[b - first], sem.at[b - first])
        for b in range(first, last)
    ]
    for c in copies:
        c.start()
    bring.wait()
    for i, c in enumerate(copies):
        c.wait()
        value = jnp.dot(hid_ref[...], buf[i], preferred_element_type=jnp.float32)
        store_outs(value, outs, i * PAIR)


def merge_kernel(mix_ref, *refs):
    ins, outs = refs[:4], refs[5:]
    got = jnp.concatenate(
        [ins[k][s].astype(jnp.float32) for k in range(N) for s in range(SLOTS)], axis=0
    ).astype(jnp.bfloat16)
    value = jnp.dot(
        mix_ref[...].astype(jnp.bfloat16), got, preferred_element_type=jnp.float32
    )
    for q in range(N):
        outs[q][...] = value[q * 4 : q * 4 + 4].astype(jnp.bfloat16)


def draw_kernel(dither_ref, _, out_ref):
    draw = dither_ref[...].astype(jnp.float32)
    at = lax.broadcasted_iota(jnp.int32, draw.shape, 1)
    for q in range(N):
        mine = jnp.where(at == (lax.axis_index("row") ^ q), draw, 0.0)
        out_ref[q] = (jnp.sum(mine, axis=1) - 0.5).astype(out_ref.dtype)


def final_kernel(chunks, draw_ref, *refs):
    ins, out_ref = refs[:-1], refs[-1]
    total = None
    for q in range(N):
        part = jnp.concatenate(
            [ins[c * N + q][...].astype(jnp.float32) for c in range(chunks)], axis=1
        )
        spread = 0.125 * jnp.max(jnp.abs(part), axis=1, keepdims=True)
        part = part + spread * draw_ref[q]
        total = part if total is None else total + part
    out_ref[...] = total.astype(jnp.bfloat16)


def local_grid(tokens, expert_ids, route_weight, dither, gate_proj, up_proj, down_proj):
    gate, up, down = gate_proj[0, 0], up_proj[0, 0], down_proj[0, 0]
    width, wide = gate.shape
    deep = down.shape[0]
    bf = jnp.bfloat16
    shape = jax.ShapeDtypeStruct
    anyw = pl.BlockSpec(memory_space=pl.ANY)
    pin = lambda a: pltpu.with_memory_space_constraint(a, pltpu.VMEM)

    packed = pl.pallas_call(
        pack_kernel,
        out_shape=shape((4, width + LANES), bf),
        in_specs=[HBM] * 4,
        out_specs=VMEM,
        scratch_shapes=[
            pltpu.VMEM((4, 8), jnp.int32),
            pltpu.VMEM((4, 8), bf),
            pltpu.SemaphoreType.DMA((3,)),
        ],
        compiler_params=params(6),
        name="pack",
    )(*(pltpu.with_memory_space_constraint(a, pltpu.HBM) for a in (tokens, expert_ids, route_weight, up)))
    near = [packed] + [lax.ppermute(packed, "col", flip(N, k)) for k in (1, 2, 3)]

    hbm = lambda a: pltpu.with_memory_space_constraint(a, pltpu.HBM)
    own = pl.pallas_call(
        stack_kernel,
        out_shape=shape((16, width + LANES), bf),
        in_specs=[VMEM] * 4 + [HBM],
        out_specs=VMEM,
        compiler_params=params(6),
        name="stack",
    )(*near, hbm(up))
    by_core = lax.ppermute(own, "row", flip(N, 1))
    by_x = lax.ppermute(own, "row", flip(N, 2))
    by_both = lax.ppermute(by_x, "row", flip(N, 1))

    chunks = (8, 6)
    outs = [shape((SLOTS, N, n * PAIR), bf) for n in chunks]
    first = pl.pallas_call(
        functools.partial(hidden_kernel, chunks[0]),
        out_shape=[outs[0]] * 4 + [shape((PACKED, wide), bf), shape((16, PACKED), jnp.float32)],
        in_specs=[anyw] * 4 + [VMEM] + [HBM] * 2,
        out_specs=[VMEM] * 6,
        scratch_shapes=[
            pltpu.VMEM((2 * ROWS, width + LANES), bf),
            pltpu.VMEM((ROWS, wide), bf),
            pltpu.VMEM((HELD, width, PAIR), bf),
            pltpu.SemaphoreType.DMA((N,)),
            pltpu.SemaphoreType.DMA((wide // PAIR,)),
            pltpu.SemaphoreType.DMA((chunks[0],)),
        ],
        compiler_params=params(28),
        cost_estimate=cost(2 * ROWS * width * wide * 3, 40 * MIB),
        name="hidden",
    )(own, by_core, by_x, by_both, pin(gate), hbm(up), hbm(down))
    hid, mix = first[4:6]
    parts = [first[:4]]
    parts.append(
        pl.pallas_call(
            functools.partial(down_kernel, chunks[0], chunks[0] + chunks[1]),
            out_shape=[outs[1]] * 4,
            in_specs=[anyw, HBM],
            out_specs=[VMEM] * 4,
            scratch_shapes=[
                pltpu.VMEM((chunks[1], deep, PAIR), bf),
                pltpu.VMEM((PACKED, wide), bf),
                pltpu.SemaphoreType.DMA((chunks[1],)),
                pltpu.SemaphoreType.DMA,
            ],
            compiler_params=params(28),
            cost_estimate=cost(2 * ROWS * width * wide, 10 * MIB),
            name="down",
        )(hid, pltpu.with_memory_space_constraint(down, pltpu.HBM))
    )
    finals = []
    after = mix
    for c, part in enumerate(parts):
        got = [part[0]] + [lax.ppermute(part[k], "col", flip(N, k)) for k in (1, 2, 3)]
        value = pl.pallas_call(
            merge_kernel,
            out_shape=[shape((4, chunks[c] * PAIR), bf)] * 4,
            in_specs=[VMEM] * 5 + [anyw],
            out_specs=[VMEM] * 4,
            compiler_params=params(6),
            cost_estimate=cost(0, 8 * MIB),
            name="merge",
        )(mix, *got, after)
        if c == 0:
            draws = pl.pallas_call(
                draw_kernel,
                out_shape=shape((N, 4, width), jnp.float32),
                in_specs=[VMEM, anyw],
                out_specs=VMEM,
                compiler_params=params(6),
                cost_estimate=cost(0, 8 * MIB),
                name="draws",
            )(dither, value[0])
            after = draws
        finals += [value[0]] + [lax.ppermute(value[q], "row", flip(N, q)) for q in (1, 2, 3)]
    return pl.pallas_call(
        functools.partial(final_kernel, len(chunks)),
        out_shape=shape((4, width), bf),
        in_specs=[VMEM] * (1 + len(finals)),
        out_specs=VMEM,
        compiler_params=params(6),
        name="final",
    )(draws, *finals)


def solution(mesh):
    def local(tokens, expert_ids, route_weight, dither, gate_proj, up_proj, down_proj):
        grid = (mesh.shape["row"], mesh.shape["col"]) == (N, N)
        whole_expert = gate_proj.shape[3] == FF and tokens.shape[0] == 4
        pick = local_grid if grid and whole_expert else local_any
        return pick(tokens, expert_ids, route_weight, dither, gate_proj, up_proj, down_proj)

    return jax.shard_map(
        local,
        mesh=mesh,
        in_specs=(
            P(("groups", "row", "col"), None),
            P(("groups", "row", "col"), None),
            P(("groups", "row", "col"), None),
            P(("groups", "row", "col"), None, None),
            P("row", "col", None, None),
            P("row", "col", None, None),
            P("row", "col", None, None),
        ),
        out_specs=P(("groups", "row", "col"), None),
        check_vma=False,
    )
```

```python
import functools

import jax
import jax.numpy as jnp
from jax import lax
from jax.experimental import pallas as pl
from jax.experimental.pallas import tpu as pltpu
from jax.sharding import PartitionSpec as P

FF = 2048
LANES = 128
COLS = 256
PAIR = 2 * COLS
MIB = 2**20
SCOPED = 18
VMEM = pl.BlockSpec(memory_space=pltpu.VMEM)
HBM = pl.BlockSpec(memory_space=pltpu.HBM)


def params(mib):
    return pltpu.CompilerParams(vmem_limit_bytes=int(mib * MIB))


def cost(flops, moved):
    return pl.CostEstimate(flops=flops, bytes_accessed=moved, transcendentals=0)


def flip(count, bit):
    return [(i, i ^ bit) for i in range(count)]


def expert_apply(batch, gate_local, up_local, down_local):
    flat = batch.reshape(-1, batch.shape[-1])
    gate_pre = jnp.dot(flat, gate_local, preferred_element_type=jnp.float32)
    up_pre = jnp.dot(flat, up_local, preferred_element_type=jnp.float32)
    hidden = (jax.nn.silu(gate_pre) * up_pre).astype(jnp.bfloat16)
    partial_value = jnp.dot(hidden, down_local, preferred_element_type=jnp.float32).astype(
        jnp.bfloat16
    )
    return partial_value.reshape(batch.shape)


def local_any(tokens, expert_ids, route_weight, dither, gate_proj, up_proj, down_proj):
    row_count = lax.axis_size("row")
    col_count = lax.axis_size("col")
    tok_count = tokens.shape[0]
    model_width = tokens.shape[1]
    pieces = FF // gate_proj.shape[3]
    per_row = col_count // pieces
    slot_count = 3 * tok_count // 4
    expert_count = row_count * per_row
    labels = lax.broadcasted_iota(jnp.int32, (1, 1, expert_count), 2)
    matches = expert_ids[:, :, None] == labels
    counted = jnp.sum(matches.astype(jnp.int32), axis=1)
    weighted = jnp.sum(
        jnp.where(matches, route_weight[:, :, None].astype(jnp.float32), 0.0), axis=1
    )
    before = jnp.cumsum(counted, axis=0) - counted
    slot_ids = lax.broadcasted_iota(jnp.int32, (1, 1, slot_count), 2)
    placed = (counted[:, :, None] == 1) & (before[:, :, None] == slot_ids)
    placed = placed.reshape(tok_count, row_count, per_row, slot_count)
    shares = (
        placed.astype(jnp.float32) * weighted.reshape(tok_count, row_count, per_row)[:, :, :, None]
    )
    place_bf = placed.astype(jnp.bfloat16)
    outgoing = jnp.einsum(
        "trjm,td->jrmd", place_bf, tokens, preferred_element_type=jnp.float32
    ).astype(jnp.bfloat16)
    share_out = jnp.transpose(shares, (2, 1, 3, 0)).astype(jnp.bfloat16)
    arrived, arrived_share, arrived_dither = (
        lax.all_to_all(outgoing, "row", split_axis=1, concat_axis=1, tiled=True),
        lax.all_to_all(share_out, "row", split_axis=1, concat_axis=1, tiled=True),
        lax.all_to_all(dither, "row", split_axis=1, concat_axis=1, tiled=True),
    )
    fanned = jnp.broadcast_to(arrived[:, None], (per_row, pieces) + arrived.shape[1:])
    fanned = fanned.reshape((col_count,) + arrived.shape[1:])
    returned = lax.all_to_all(
        expert_apply(
            lax.all_to_all(fanned, "col", split_axis=0, concat_axis=0, tiled=True),
            gate_proj[0, 0],
            up_proj[0, 0],
            down_proj[0, 0],
        ),
        "col",
        split_axis=0,
        concat_axis=0,
        tiled=True,
    )
    merged = jnp.sum(
        returned.reshape(per_row, pieces, row_count, slot_count, model_width).astype(jnp.float32),
        axis=1,
    )
    combined = jnp.einsum(
        "jrmt,jrmd->trd", arrived_share.astype(jnp.float32), merged, precision=lax.Precision.HIGHEST
    )
    spread = 0.125 * jnp.max(jnp.abs(combined), axis=2, keepdims=True)
    rounded = (combined + spread * (arrived_dither.astype(jnp.float32) - 0.5)).astype(jnp.bfloat16)
    collected = lax.all_to_all(rounded, "row", split_axis=1, concat_axis=1, tiled=True)
    return jnp.sum(collected.astype(jnp.float32), axis=1).astype(jnp.bfloat16)


N = 4
SLOTS = 3
BLOCKS = N * N
ROWS = BLOCKS * 4
EARLY = 1
HELD = 2
PACKED = N * SLOTS * N


def pack_kernel(tok_ref, ids_ref, share_ref, _, out_ref, ids_here, share_here, sem):
    width = tok_ref.shape[1]
    copies = [
        pltpu.make_async_copy(ids_ref, ids_here, sem.at[0]),
        pltpu.make_async_copy(share_ref, share_here, sem.at[1]),
        pltpu.make_async_copy(tok_ref, out_ref.at[:, pl.ds(0, width)], sem.at[2]),
    ]
    for c in copies:
        c.start()
    for c in copies:
        c.wait()
    tail = jnp.concatenate(
        [
            ids_here[...].astype(jnp.float32),
            share_here[...].astype(jnp.float32),
            jnp.zeros((4, LANES - 16), jnp.float32),
        ],
        axis=1,
    )
    out_ref[:, width:] = tail.astype(jnp.bfloat16)


def stack_kernel(*refs):
    out_ref, mark_ref = refs[-2:]
    mark_ref[...] = jnp.zeros_like(mark_ref)
    parts = [r[...].astype(jnp.float32) for r in refs[:4]]
    out_ref[...] = jnp.concatenate(parts, axis=0).astype(jnp.bfloat16)


def up_copy(up_ref, buf, sem, j, first):
    return pltpu.make_async_copy(
        up_ref.at[:, pl.ds(j * PAIR, PAIR)], buf.at[(j - first) % buf.shape[0]], sem.at[j]
    )


def fill_kernel(up_ref, _, buf, sem):
    copies = [up_copy(up_ref, buf, sem, j, 0) for j in range(buf.shape[0])]
    for c in copies:
        c.start()
    for c in copies:
        c.wait()


def routing(meta, me_row, me_col):
    ids, share = meta[:, :8], meta[:, 8:16]
    at = lax.broadcasted_iota(jnp.int32, (ROWS, ROWS), 0)
    to = lax.broadcasted_iota(jnp.int32, (ROWS, ROWS), 1)
    earlier = ((at // 4 == to // 4) & (to < at)).astype(jnp.bfloat16)
    found, rank, weight = [], [], []
    for k in range(N):
        expert = (me_row * N + (me_col ^ k)).astype(jnp.float32)
        hit = (ids == expert).astype(jnp.float32)
        found.append(jnp.sum(hit, axis=1, keepdims=True))
        weight.append(jnp.sum(hit * share, axis=1, keepdims=True))
    lanes = jnp.concatenate(found + [jnp.zeros((ROWS, LANES - N), jnp.float32)], axis=1)
    rank = jnp.dot(earlier, lanes.astype(jnp.bfloat16), preferred_element_type=jnp.float32)
    return found, rank, weight


def store_outs(value, outs, lo):
    width = value.shape[1]
    for k in range(N):
        for s in range(SLOTS):
            at = (k * SLOTS + s) * N
            outs[k][s, :, lo : lo + width] = value[at : at + N].astype(jnp.bfloat16)


def hidden_kernel(blocks, *refs):
    pieces = refs[:4]
    gate_ref, up_ref, down_ref, early_ref = refs[4:8]
    outs, hid_ref, mix_ref = refs[8:12], refs[12], refs[13]
    x_ref, h_ref, buf, piece_sem, fill_sem, down_sem = refs[14:]
    early = early_ref.shape[0]
    width = gate_ref.shape[0]
    deep = down_ref.shape[0]
    steps = deep // PAIR
    bring = [
        pltpu.make_async_copy(pieces[q], x_ref.at[pl.ds(q * 16, 16)], piece_sem.at[q])
        for q in range(N)
    ]
    for c in bring:
        c.start()
    for j in range(early, early + buf.shape[0]):
        up_copy(up_ref, buf, fill_sem, j, early).start()
    x_ref[ROWS:, :] = jnp.zeros((x_ref.shape[0] - ROWS, x_ref.shape[1]), x_ref.dtype)
    for c in bring:
        c.wait()

    def down_place(b):
        slot = (steps - early + b // 3) % buf.shape[0]
        return buf.at[slot, pl.ds(b % 3 * deep, deep)]

    def down_copy(b):
        return pltpu.make_async_copy(
            down_ref.at[:, pl.ds(b * PAIR, PAIR)], down_place(b), down_sem.at[b]
        )

    def load_next(used):
        j = used + early + buf.shape[0]
        if j < steps:
            up_copy(up_ref, buf, fill_sem, j, early).start()
            return
        first = 3 * (j - steps)
        for b in range(first, min(first + 3, blocks)):
            down_copy(b).start()

    for j in range(steps):
        at = pl.ds(j * PAIR, PAIR)
        g = jnp.dot(x_ref[:, :width], gate_ref[:, at], preferred_element_type=jnp.float32)[:ROWS]
        if j >= early:
            up_copy(up_ref, buf, fill_sem, j, early).wait()
        right = early_ref[j] if j < early else buf[(j - early) % buf.shape[0]]
        u = jnp.dot(x_ref[:, :width], right, preferred_element_type=jnp.float32)[:ROWS]
        h_ref[:, at] = (g / (1.0 + jnp.exp(-g)) * u).astype(jnp.bfloat16)
        if j >= early:
            load_next(j - early)

    meta = x_ref[:ROWS, width:].astype(jnp.float32)
    found, rank, weight = routing(meta, lax.axis_index("row"), lax.axis_index("col"))
    m_at = lax.broadcasted_iota(jnp.int32, (ROWS, PACKED), 0)
    c_at = lax.broadcasted_iota(jnp.int32, (ROWS, PACKED), 1)
    same = (m_at // 16 == c_at % 4) & ((m_at // 4) % 4 == c_at // 12)
    slot = ((c_at // 4) % 3).astype(jnp.float32)
    take = jnp.where(same & (found[0] > 0) & (rank[:, 0:1] == slot), 1.0, 0.0)
    hid = lax.dot_general(
        take.astype(jnp.bfloat16),
        h_ref[...],
        (((0,), (0,)), ((), ())),
        preferred_element_type=jnp.float32,
    )
    hid_ref[...] = hid.astype(jnp.bfloat16)
    mix = jnp.zeros((ROWS, PACKED), jnp.float32)
    for k in range(N):
        here = (c_at // 12 == k) & (m_at // 16 == c_at % 4)
        mix = jnp.where(here & (found[k] > 0) & (rank[:, k : k + 1] == slot), weight[k], mix)
    for q in range(N):
        mix_ref[q * 4 : q * 4 + 4, :] = mix[q * 16 : q * 16 + 4]
    for b in range(blocks):
        down_copy(b).wait()
        value = jnp.dot(
            hid_ref[...],
            down_place(b)[...],
            preferred_element_type=jnp.float32,
        )
        store_outs(value, outs, b * PAIR)
        if b % 3 == 2:
            load_next(steps - early + b // 3)


def down_kernel(first, last, hid_from, down_ref, *refs):
    outs, buf, hid_ref, sem, hid_sem = refs[:4], refs[4], refs[5], refs[6], refs[7]
    bring = pltpu.make_async_copy(hid_from, hid_ref, hid_sem)
    bring.start()
    copies = [
        pltpu.make_async_copy(down_ref.at[:, pl.ds(b * PAIR, PAIR)], buf.at[b - first], sem.at[b - first])
        for b in range(first, last)
    ]
    for c in copies:
        c.start()
    bring.wait()
    for i, c in enumerate(copies):
        c.wait()
        value = jnp.dot(hid_ref[...], buf[i], preferred_element_type=jnp.float32)
        store_outs(value, outs, i * PAIR)


def merge_kernel(mix_ref, *refs):
    ins, outs = refs[:4], refs[-4:]
    got = jnp.concatenate(
        [ins[k][s].astype(jnp.float32) for k in range(N) for s in range(SLOTS)], axis=0
    ).astype(jnp.bfloat16)
    value = jnp.dot(
        mix_ref[...].astype(jnp.bfloat16), got, preferred_element_type=jnp.float32
    )
    for q in range(N):
        outs[q][...] = value[q * 4 : q * 4 + 4].astype(jnp.bfloat16)


def draw_kernel(dither_ref, _, out_ref):
    draw = dither_ref[...].astype(jnp.float32)
    at = lax.broadcasted_iota(jnp.int32, draw.shape, 1)
    for q in range(N):
        mine = jnp.where(at == (lax.axis_index("row") ^ q), draw, 0.0)
        out_ref[q] = (jnp.sum(mine, axis=1) - 0.5).astype(out_ref.dtype)


def final_kernel(chunks, draw_ref, *refs):
    ins, out_ref = refs[:-1], refs[-1]
    total = None
    for q in range(N):
        part = jnp.concatenate(
            [ins[c * N + q][...].astype(jnp.float32) for c in range(chunks)], axis=1
        )
        spread = 0.125 * jnp.max(jnp.abs(part), axis=1, keepdims=True)
        part = part + spread * draw_ref[q]
        total = part if total is None else total + part
    out_ref[...] = total.astype(jnp.bfloat16)


def local_grid(tokens, expert_ids, route_weight, dither, gate_proj, up_proj, down_proj):
    gate, up, down = gate_proj[0, 0], up_proj[0, 0], down_proj[0, 0]
    width, wide = gate.shape
    deep = down.shape[0]
    bf = jnp.bfloat16
    shape = jax.ShapeDtypeStruct
    anyw = pl.BlockSpec(memory_space=pl.ANY)
    pin = lambda a: pltpu.with_memory_space_constraint(a, pltpu.VMEM)

    packed = pl.pallas_call(
        pack_kernel,
        out_shape=shape((4, width + LANES), bf),
        in_specs=[HBM] * 4,
        out_specs=VMEM,
        scratch_shapes=[
            pltpu.VMEM((4, 8), jnp.int32),
            pltpu.VMEM((4, 8), bf),
            pltpu.SemaphoreType.DMA((3,)),
        ],
        compiler_params=params(6),
        name="pack",
    )(*(pltpu.with_memory_space_constraint(a, pltpu.HBM) for a in (tokens, expert_ids, route_weight, up)))
    near = [packed] + [lax.ppermute(packed, "col", flip(N, k)) for k in (1, 2, 3)]

    hbm = lambda a: pltpu.with_memory_space_constraint(a, pltpu.HBM)
    own, mark = pl.pallas_call(
        stack_kernel,
        out_shape=[shape((16, width + LANES), bf), shape((8, LANES), jnp.float32)],
        in_specs=[VMEM] * 4 + [HBM],
        out_specs=[VMEM] * 2,
        compiler_params=params(6),
        name="stack",
    )(*near, hbm(up))
    by_core = lax.ppermute(own, "row", flip(N, 1))
    by_x = lax.ppermute(own, "row", flip(N, 2))
    early = pl.pallas_call(
        fill_kernel,
        out_shape=pltpu.VMEM((EARLY, width, PAIR), bf),
        in_specs=[HBM, anyw],
        out_specs=VMEM,
        scratch_shapes=[pltpu.SemaphoreType.DMA((EARLY,))],
        compiler_params=params(SCOPED),
        cost_estimate=cost(0, EARLY * width * PAIR * 2),
        name="fill",
    )(hbm(up), mark)
    by_x, early = lax.optimization_barrier((by_x, early))
    by_both = lax.ppermute(by_x, "row", flip(N, 1))

    chunks = (8, 6)
    outs = [shape((SLOTS, N, n * PAIR), bf) for n in chunks]
    first = pl.pallas_call(
        functools.partial(hidden_kernel, chunks[0]),
        out_shape=[outs[0]] * 4 + [pltpu.VMEM((PACKED, wide), bf), pltpu.VMEM((16, PACKED), jnp.float32)],
        in_specs=[anyw] * 4 + [VMEM] + [HBM] * 2 + [VMEM],
        out_specs=[VMEM] * 6,
        scratch_shapes=[
            pltpu.VMEM((2 * ROWS, width + LANES), bf),
            pltpu.VMEM((ROWS, wide), bf),
            pltpu.VMEM((HELD, width, PAIR), bf),
            pltpu.SemaphoreType.DMA((N,)),
            pltpu.SemaphoreType.DMA((wide // PAIR,)),
            pltpu.SemaphoreType.DMA((chunks[0],)),
        ],
        compiler_params=params(SCOPED),
        cost_estimate=cost(2 * ROWS * width * wide * 3, 40 * MIB),
        name="hidden",
    )(own, by_core, by_x, by_both, pin(gate), hbm(up), hbm(down), pin(early))
    hid, mix = first[4:6]
    parts = [first[:4]]
    parts.append(
        pl.pallas_call(
            functools.partial(down_kernel, chunks[0], chunks[0] + chunks[1]),
            out_shape=[outs[1]] * 4,
            in_specs=[anyw, HBM],
            out_specs=[VMEM] * 4,
            scratch_shapes=[
                pltpu.VMEM((chunks[1], deep, PAIR), bf),
                pltpu.VMEM((PACKED, wide), bf),
                pltpu.SemaphoreType.DMA((chunks[1],)),
                pltpu.SemaphoreType.DMA,
            ],
            compiler_params=params(28),
            cost_estimate=cost(2 * ROWS * width * wide, 10 * MIB),
            name="down",
        )(hid, pltpu.with_memory_space_constraint(down, pltpu.HBM))
    )
    finals = []
    after = []
    for c, part in enumerate(parts):
        got = [part[0]] + [lax.ppermute(part[k], "col", flip(N, k)) for k in (1, 2, 3)]
        value = pl.pallas_call(
            merge_kernel,
            out_shape=[shape((4, chunks[c] * PAIR), bf)] * 4,
            in_specs=[VMEM] * 5 + [anyw] * len(after),
            out_specs=[VMEM] * 4,
            compiler_params=params(6),
            cost_estimate=cost(0, 8 * MIB),
            name="merge",
        )(mix, *got, *after)
        if c == 0:
            draws = pl.pallas_call(
                draw_kernel,
                out_shape=shape((N, 4, width), jnp.float32),
                in_specs=[VMEM, anyw],
                out_specs=VMEM,
                compiler_params=params(6),
                cost_estimate=cost(0, 8 * MIB),
                name="draws",
            )(dither, value[0])
        sent = [lax.ppermute(value[q], "row", flip(N, q)) for q in (1, 2, 3)]
        finals += [value[0]] + sent
        after = [draws] + sent
    return pl.pallas_call(
        functools.partial(final_kernel, len(chunks)),
        out_shape=shape((4, width), bf),
        in_specs=[VMEM] * (1 + len(finals)),
        out_specs=VMEM,
        compiler_params=params(6),
        name="final",
    )(draws, *finals)


def solution(mesh):
    def local(tokens, expert_ids, route_weight, dither, gate_proj, up_proj, down_proj):
        grid = (mesh.shape["row"], mesh.shape["col"]) == (N, N)
        whole_expert = gate_proj.shape[3] == FF and tokens.shape[0] == 4
        pick = local_grid if grid and whole_expert else local_any
        return pick(tokens, expert_ids, route_weight, dither, gate_proj, up_proj, down_proj)

    return jax.shard_map(
        local,
        mesh=mesh,
        in_specs=(
            P(("groups", "row", "col"), None),
            P(("groups", "row", "col"), None),
            P(("groups", "row", "col"), None),
            P(("groups", "row", "col"), None, None),
            P("row", "col", None, None),
            P("row", "col", None, None),
            P("row", "col", None, None),
        ),
        out_specs=P(("groups", "row", "col"), None),
        check_vma=False,
    )
```

```python
import functools

import jax
import jax.numpy as jnp
from jax import lax
from jax.experimental import pallas as pl
from jax.experimental.pallas import tpu as pltpu
from jax.sharding import PartitionSpec as P

FF = 2048
LANES = 128
COLS = 256
PAIR = 2 * COLS
MIB = 2**20
SCOPED = 17.3
VMEM = pl.BlockSpec(memory_space=pltpu.VMEM)
HBM = pl.BlockSpec(memory_space=pltpu.HBM)


def params(mib):
    return pltpu.CompilerParams(vmem_limit_bytes=int(mib * MIB))


def cost(flops, moved):
    return pl.CostEstimate(flops=flops, bytes_accessed=moved, transcendentals=0)


def flip(count, bit):
    return [(i, i ^ bit) for i in range(count)]


def expert_apply(batch, gate_local, up_local, down_local):
    flat = batch.reshape(-1, batch.shape[-1])
    gate_pre = jnp.dot(flat, gate_local, preferred_element_type=jnp.float32)
    up_pre = jnp.dot(flat, up_local, preferred_element_type=jnp.float32)
    hidden = (jax.nn.silu(gate_pre) * up_pre).astype(jnp.bfloat16)
    partial_value = jnp.dot(hidden, down_local, preferred_element_type=jnp.float32).astype(
        jnp.bfloat16
    )
    return partial_value.reshape(batch.shape)


def local_any(tokens, expert_ids, route_weight, dither, gate_proj, up_proj, down_proj):
    row_count = lax.axis_size("row")
    col_count = lax.axis_size("col")
    tok_count = tokens.shape[0]
    model_width = tokens.shape[1]
    pieces = FF // gate_proj.shape[3]
    per_row = col_count // pieces
    slot_count = 3 * tok_count // 4
    expert_count = row_count * per_row
    labels = lax.broadcasted_iota(jnp.int32, (1, 1, expert_count), 2)
    matches = expert_ids[:, :, None] == labels
    counted = jnp.sum(matches.astype(jnp.int32), axis=1)
    weighted = jnp.sum(
        jnp.where(matches, route_weight[:, :, None].astype(jnp.float32), 0.0), axis=1
    )
    before = jnp.cumsum(counted, axis=0) - counted
    slot_ids = lax.broadcasted_iota(jnp.int32, (1, 1, slot_count), 2)
    placed = (counted[:, :, None] == 1) & (before[:, :, None] == slot_ids)
    placed = placed.reshape(tok_count, row_count, per_row, slot_count)
    shares = (
        placed.astype(jnp.float32) * weighted.reshape(tok_count, row_count, per_row)[:, :, :, None]
    )
    place_bf = placed.astype(jnp.bfloat16)
    outgoing = jnp.einsum(
        "trjm,td->jrmd", place_bf, tokens, preferred_element_type=jnp.float32
    ).astype(jnp.bfloat16)
    share_out = jnp.transpose(shares, (2, 1, 3, 0)).astype(jnp.bfloat16)
    arrived, arrived_share, arrived_dither = (
        lax.all_to_all(outgoing, "row", split_axis=1, concat_axis=1, tiled=True),
        lax.all_to_all(share_out, "row", split_axis=1, concat_axis=1, tiled=True),
        lax.all_to_all(dither, "row", split_axis=1, concat_axis=1, tiled=True),
    )
    fanned = jnp.broadcast_to(arrived[:, None], (per_row, pieces) + arrived.shape[1:])
    fanned = fanned.reshape((col_count,) + arrived.shape[1:])
    returned = lax.all_to_all(
        expert_apply(
            lax.all_to_all(fanned, "col", split_axis=0, concat_axis=0, tiled=True),
            gate_proj[0, 0],
            up_proj[0, 0],
            down_proj[0, 0],
        ),
        "col",
        split_axis=0,
        concat_axis=0,
        tiled=True,
    )
    merged = jnp.sum(
        returned.reshape(per_row, pieces, row_count, slot_count, model_width).astype(jnp.float32),
        axis=1,
    )
    combined = jnp.einsum(
        "jrmt,jrmd->trd", arrived_share.astype(jnp.float32), merged, precision=lax.Precision.HIGHEST
    )
    spread = 0.125 * jnp.max(jnp.abs(combined), axis=2, keepdims=True)
    rounded = (combined + spread * (arrived_dither.astype(jnp.float32) - 0.5)).astype(jnp.bfloat16)
    collected = lax.all_to_all(rounded, "row", split_axis=1, concat_axis=1, tiled=True)
    return jnp.sum(collected.astype(jnp.float32), axis=1).astype(jnp.bfloat16)


N = 4
SLOTS = 3
BLOCKS = N * N
ROWS = BLOCKS * 4
EARLY = 1
HELD = 2
PACKED = N * SLOTS * N


def pack_kernel(tok_ref, ids_ref, share_ref, _, out_ref, ids_here, share_here, sem):
    width = tok_ref.shape[1]
    copies = [
        pltpu.make_async_copy(ids_ref, ids_here, sem.at[0]),
        pltpu.make_async_copy(share_ref, share_here, sem.at[1]),
        pltpu.make_async_copy(tok_ref, out_ref.at[:, pl.ds(0, width)], sem.at[2]),
    ]
    for c in copies:
        c.start()
    for c in copies:
        c.wait()
    tail = jnp.concatenate(
        [
            ids_here[...].astype(jnp.float32),
            share_here[...].astype(jnp.float32),
            jnp.zeros((4, LANES - 16), jnp.float32),
        ],
        axis=1,
    )
    out_ref[:, width:] = tail.astype(jnp.bfloat16)


def stack_kernel(*refs):
    out_ref, mark_ref = refs[-2:]
    mark_ref[...] = jnp.zeros_like(mark_ref)
    parts = [r[...].astype(jnp.float32) for r in refs[:4]]
    out_ref[...] = jnp.concatenate(parts, axis=0).astype(jnp.bfloat16)


def up_copy(up_ref, buf, sem, j, first):
    return pltpu.make_async_copy(
        up_ref.at[:, pl.ds(j * PAIR, PAIR)], buf.at[(j - first) % buf.shape[0]], sem.at[j]
    )


def fill_kernel(up_ref, _, buf, sem):
    copies = [up_copy(up_ref, buf, sem, j, 0) for j in range(buf.shape[0])]
    for c in copies:
        c.start()
    for c in copies:
        c.wait()


def routing(meta, me_row, me_col):
    ids, share = meta[:, :8], meta[:, 8:16]
    at = lax.broadcasted_iota(jnp.int32, (ROWS, ROWS), 0)
    to = lax.broadcasted_iota(jnp.int32, (ROWS, ROWS), 1)
    earlier = ((at // 4 == to // 4) & (to < at)).astype(jnp.bfloat16)
    found, rank, weight = [], [], []
    for k in range(N):
        expert = (me_row * N + (me_col ^ k)).astype(jnp.float32)
        hit = (ids == expert).astype(jnp.float32)
        found.append(jnp.sum(hit, axis=1, keepdims=True))
        weight.append(jnp.sum(hit * share, axis=1, keepdims=True))
    lanes = jnp.concatenate(found + [jnp.zeros((ROWS, LANES - N), jnp.float32)], axis=1)
    rank = jnp.dot(earlier, lanes.astype(jnp.bfloat16), preferred_element_type=jnp.float32)
    return found, rank, weight


def store_outs(value, outs, lo):
    width = value.shape[1]
    for k in range(N):
        for s in range(SLOTS):
            at = (k * SLOTS + s) * N
            outs[k][s, :, lo : lo + width] = value[at : at + N].astype(jnp.bfloat16)


def hidden_kernel(blocks, *refs):
    pieces = refs[:4]
    gate_ref, up_ref, down_ref, early_ref = refs[4:8]
    outs, hid_ref, mix_ref = refs[8:12], refs[12], refs[13]
    x_ref, h_ref, buf, piece_sem, fill_sem, down_sem = refs[14:]
    early = early_ref.shape[0]
    width = gate_ref.shape[0]
    deep = down_ref.shape[0]
    steps = deep // PAIR
    bring = [
        pltpu.make_async_copy(pieces[q], x_ref.at[pl.ds(q * 16, 16)], piece_sem.at[q])
        for q in range(N)
    ]
    for c in bring:
        c.start()
    for j in range(early, early + buf.shape[0]):
        up_copy(up_ref, buf, fill_sem, j, early).start()
    x_ref[ROWS:, :] = jnp.zeros((x_ref.shape[0] - ROWS, x_ref.shape[1]), x_ref.dtype)
    for c in bring:
        c.wait()

    def down_place(b):
        slot = (steps - early + b // 3) % buf.shape[0]
        return buf.at[slot, pl.ds(b % 3 * deep, deep)]

    def down_copy(b):
        return pltpu.make_async_copy(
            down_ref.at[:, pl.ds(b * PAIR, PAIR)], down_place(b), down_sem.at[b]
        )

    def load_next(used):
        j = used + early + buf.shape[0]
        if j < steps:
            up_copy(up_ref, buf, fill_sem, j, early).start()
            return
        first = 3 * (j - steps)
        for b in range(first, min(first + 3, blocks)):
            down_copy(b).start()

    for j in range(steps):
        at = pl.ds(j * PAIR, PAIR)
        g = jnp.dot(x_ref[:, :width], gate_ref[:, at], preferred_element_type=jnp.float32)[:ROWS]
        if j >= early:
            up_copy(up_ref, buf, fill_sem, j, early).wait()
        right = early_ref[j] if j < early else buf[(j - early) % buf.shape[0]]
        u = jnp.dot(x_ref[:, :width], right, preferred_element_type=jnp.float32)[:ROWS]
        h_ref[:, at] = (g / (1.0 + jnp.exp(-g)) * u).astype(jnp.bfloat16)
        if j >= early:
            load_next(j - early)

    meta = x_ref[:ROWS, width:].astype(jnp.float32)
    found, rank, weight = routing(meta, lax.axis_index("row"), lax.axis_index("col"))
    m_at = lax.broadcasted_iota(jnp.int32, (ROWS, PACKED), 0)
    c_at = lax.broadcasted_iota(jnp.int32, (ROWS, PACKED), 1)
    same = (m_at // 16 == c_at % 4) & ((m_at // 4) % 4 == c_at // 12)
    slot = ((c_at // 4) % 3).astype(jnp.float32)
    take = jnp.where(same & (found[0] > 0) & (rank[:, 0:1] == slot), 1.0, 0.0)
    hid = lax.dot_general(
        take.astype(jnp.bfloat16),
        h_ref[...],
        (((0,), (0,)), ((), ())),
        preferred_element_type=jnp.float32,
    )
    hid_ref[...] = hid.astype(jnp.bfloat16)
    mix = jnp.zeros((ROWS, PACKED), jnp.float32)
    for k in range(N):
        here = (c_at // 12 == k) & (m_at // 16 == c_at % 4)
        mix = jnp.where(here & (found[k] > 0) & (rank[:, k : k + 1] == slot), weight[k], mix)
    for q in range(N):
        mix_ref[q * 4 : q * 4 + 4, :] = mix[q * 16 : q * 16 + 4]
    for b in range(blocks):
        down_copy(b).wait()
        value = jnp.dot(
            hid_ref[...],
            down_place(b)[...],
            preferred_element_type=jnp.float32,
        )
        store_outs(value, outs, b * PAIR)
        if b % 3 == 2:
            load_next(steps - early + b // 3)


def down_kernel(first, last, hid_from, down_ref, *refs):
    outs, buf, hid_ref, sem, hid_sem = refs[:4], refs[4], refs[5], refs[6], refs[7]
    bring = pltpu.make_async_copy(hid_from, hid_ref, hid_sem)
    bring.start()
    copies = [
        pltpu.make_async_copy(down_ref.at[:, pl.ds(b * PAIR, PAIR)], buf.at[b - first], sem.at[b - first])
        for b in range(first, last)
    ]
    for c in copies:
        c.start()
    bring.wait()
    for i, c in enumerate(copies):
        c.wait()
        value = jnp.dot(hid_ref[...], buf[i], preferred_element_type=jnp.float32)
        store_outs(value, outs, i * PAIR)


def merge_kernel(mix_ref, *refs):
    ins, outs = refs[:4], refs[-4:]
    got = jnp.concatenate(
        [ins[k][s].astype(jnp.float32) for k in range(N) for s in range(SLOTS)], axis=0
    ).astype(jnp.bfloat16)
    value = jnp.dot(
        mix_ref[...].astype(jnp.bfloat16), got, preferred_element_type=jnp.float32
    )
    for q in range(N):
        outs[q][...] = value[q * 4 : q * 4 + 4].astype(jnp.bfloat16)


def draw_kernel(dither_ref, _, out_ref):
    draw = dither_ref[...].astype(jnp.float32)
    at = lax.broadcasted_iota(jnp.int32, draw.shape, 1)
    for q in range(N):
        mine = jnp.where(at == (lax.axis_index("row") ^ q), draw, 0.0)
        out_ref[q] = (jnp.sum(mine, axis=1) - 0.5).astype(out_ref.dtype)


def final_kernel(chunks, draw_ref, *refs):
    ins, out_ref = refs[:-1], refs[-1]
    total = None
    for q in range(N):
        part = jnp.concatenate(
            [ins[c * N + q][...].astype(jnp.float32) for c in range(chunks)], axis=1
        )
        spread = 0.125 * jnp.max(jnp.abs(part), axis=1, keepdims=True)
        part = part + spread * draw_ref[q]
        total = part if total is None else total + part
    out_ref[...] = total.astype(jnp.bfloat16)


def local_grid(tokens, expert_ids, route_weight, dither, gate_proj, up_proj, down_proj):
    gate, up, down = gate_proj[0, 0], up_proj[0, 0], down_proj[0, 0]
    width, wide = gate.shape
    deep = down.shape[0]
    bf = jnp.bfloat16
    shape = jax.ShapeDtypeStruct
    anyw = pl.BlockSpec(memory_space=pl.ANY)
    pin = lambda a: pltpu.with_memory_space_constraint(a, pltpu.VMEM)

    packed = pl.pallas_call(
        pack_kernel,
        out_shape=shape((4, width + LANES), bf),
        in_specs=[HBM] * 4,
        out_specs=VMEM,
        scratch_shapes=[
            pltpu.VMEM((4, 8), jnp.int32),
            pltpu.VMEM((4, 8), bf),
            pltpu.SemaphoreType.DMA((3,)),
        ],
        compiler_params=params(6),
        name="pack",
    )(*(pltpu.with_memory_space_constraint(a, pltpu.HBM) for a in (tokens, expert_ids, route_weight, up)))
    near = [packed] + [lax.ppermute(packed, "col", flip(N, k)) for k in (1, 2, 3)]

    hbm = lambda a: pltpu.with_memory_space_constraint(a, pltpu.HBM)
    own, mark = pl.pallas_call(
        stack_kernel,
        out_shape=[shape((16, width + LANES), bf), shape((8, LANES), jnp.float32)],
        in_specs=[VMEM] * 4 + [HBM],
        out_specs=[VMEM] * 2,
        compiler_params=params(6),
        name="stack",
    )(*near, hbm(up))
    by_core = lax.ppermute(own, "row", flip(N, 1))
    by_x = lax.ppermute(own, "row", flip(N, 2))
    early = pl.pallas_call(
        fill_kernel,
        out_shape=pltpu.VMEM((EARLY, width, PAIR), bf),
        in_specs=[HBM, anyw],
        out_specs=VMEM,
        scratch_shapes=[pltpu.SemaphoreType.DMA((EARLY,))],
        compiler_params=params(SCOPED),
        cost_estimate=cost(0, EARLY * width * PAIR * 2),
        name="fill",
    )(hbm(up), mark)
    by_x, early = lax.optimization_barrier((by_x, early))
    by_both = lax.ppermute(by_x, "row", flip(N, 1))

    chunks = (8, 6)
    outs = [shape((SLOTS, N, n * PAIR), bf) for n in chunks]
    first = pl.pallas_call(
        functools.partial(hidden_kernel, chunks[0]),
        out_shape=[outs[0]] * 4 + [pltpu.VMEM((PACKED, wide), bf), pltpu.VMEM((16, PACKED), jnp.float32)],
        in_specs=[anyw] * 4 + [VMEM] + [HBM] * 2 + [VMEM],
        out_specs=[VMEM] * 6,
        scratch_shapes=[
            pltpu.VMEM((2 * ROWS, width + LANES), bf),
            pltpu.VMEM((ROWS, wide), bf),
            pltpu.VMEM((HELD, width, PAIR), bf),
            pltpu.SemaphoreType.DMA((N,)),
            pltpu.SemaphoreType.DMA((wide // PAIR,)),
            pltpu.SemaphoreType.DMA((chunks[0],)),
        ],
        compiler_params=params(SCOPED),
        cost_estimate=cost(2 * ROWS * width * wide * 3, 40 * MIB),
        name="hidden",
    )(own, by_core, by_x, by_both, pin(gate), hbm(up), hbm(down), pin(early))
    hid, mix = first[4:6]
    parts = [first[:4]]
    parts.append(
        pl.pallas_call(
            functools.partial(down_kernel, chunks[0], chunks[0] + chunks[1]),
            out_shape=[outs[1]] * 4,
            in_specs=[anyw, HBM],
            out_specs=[VMEM] * 4,
            scratch_shapes=[
                pltpu.VMEM((chunks[1], deep, PAIR), bf),
                pltpu.VMEM((PACKED, wide), bf),
                pltpu.SemaphoreType.DMA((chunks[1],)),
                pltpu.SemaphoreType.DMA,
            ],
            compiler_params=params(28),
            cost_estimate=cost(2 * ROWS * width * wide, 10 * MIB),
            name="down",
        )(hid, pltpu.with_memory_space_constraint(down, pltpu.HBM))
    )
    finals = []
    after = []
    for c, part in enumerate(parts):
        got = [part[0]] + [lax.ppermute(part[k], "col", flip(N, k)) for k in (1, 2, 3)]
        value = pl.pallas_call(
            merge_kernel,
            out_shape=[shape((4, chunks[c] * PAIR), bf)] * 4,
            in_specs=[VMEM] * 5 + [anyw] * len(after),
            out_specs=[VMEM] * 4,
            compiler_params=params(6),
            cost_estimate=cost(0, 8 * MIB),
            name="merge",
        )(mix, *got, *after)
        if c == 0:
            draws = pl.pallas_call(
                draw_kernel,
                out_shape=shape((N, 4, width), jnp.float32),
                in_specs=[VMEM, anyw],
                out_specs=VMEM,
                compiler_params=params(6),
                cost_estimate=cost(0, 8 * MIB),
                name="draws",
            )(dither, value[0])
        sent = [lax.ppermute(value[q], "row", flip(N, q)) for q in (1, 2, 3)]
        finals += [value[0]] + sent
        after = [draws] + sent
    return pl.pallas_call(
        functools.partial(final_kernel, len(chunks)),
        out_shape=shape((4, width), bf),
        in_specs=[VMEM] * (1 + len(finals)),
        out_specs=VMEM,
        compiler_params=params(6),
        name="final",
    )(draws, *finals)


def solution(mesh):
    def local(tokens, expert_ids, route_weight, dither, gate_proj, up_proj, down_proj):
        grid = (mesh.shape["row"], mesh.shape["col"]) == (N, N)
        whole_expert = gate_proj.shape[3] == FF and tokens.shape[0] == 4
        pick = local_grid if grid and whole_expert else local_any
        return pick(tokens, expert_ids, route_weight, dither, gate_proj, up_proj, down_proj)

    return jax.shard_map(
        local,
        mesh=mesh,
        in_specs=(
            P(("groups", "row", "col"), None),
            P(("groups", "row", "col"), None),
            P(("groups", "row", "col"), None),
            P(("groups", "row", "col"), None, None),
            P("row", "col", None, None),
            P("row", "col", None, None),
            P("row", "col", None, None),
        ),
        out_specs=P(("groups", "row", "col"), None),
        check_vma=False,
    )
```

```python
import functools

import jax
import jax.numpy as jnp
from jax import lax
from jax.experimental import pallas as pl
from jax.experimental.pallas import tpu as pltpu
from jax.sharding import PartitionSpec as P

FF = 2048
LANES = 128
COLS = 256
PAIR = 2 * COLS
MIB = 2**20
SCOPED = 17.3
VMEM = pl.BlockSpec(memory_space=pltpu.VMEM)
HBM = pl.BlockSpec(memory_space=pltpu.HBM)


def params(mib):
    return pltpu.CompilerParams(vmem_limit_bytes=int(mib * MIB))


def cost(flops, moved):
    return pl.CostEstimate(flops=flops, bytes_accessed=moved, transcendentals=0)


def flip(count, bit):
    return [(i, i ^ bit) for i in range(count)]


def expert_apply(batch, gate_local, up_local, down_local):
    flat = batch.reshape(-1, batch.shape[-1])
    gate_pre = jnp.dot(flat, gate_local, preferred_element_type=jnp.float32)
    up_pre = jnp.dot(flat, up_local, preferred_element_type=jnp.float32)
    hidden = (jax.nn.silu(gate_pre) * up_pre).astype(jnp.bfloat16)
    partial_value = jnp.dot(hidden, down_local, preferred_element_type=jnp.float32).astype(
        jnp.bfloat16
    )
    return partial_value.reshape(batch.shape)


def local_any(tokens, expert_ids, route_weight, dither, gate_proj, up_proj, down_proj):
    row_count = lax.axis_size("row")
    col_count = lax.axis_size("col")
    tok_count = tokens.shape[0]
    model_width = tokens.shape[1]
    pieces = FF // gate_proj.shape[3]
    per_row = col_count // pieces
    slot_count = 3 * tok_count // 4
    expert_count = row_count * per_row
    labels = lax.broadcasted_iota(jnp.int32, (1, 1, expert_count), 2)
    matches = expert_ids[:, :, None] == labels
    counted = jnp.sum(matches.astype(jnp.int32), axis=1)
    weighted = jnp.sum(
        jnp.where(matches, route_weight[:, :, None].astype(jnp.float32), 0.0), axis=1
    )
    before = jnp.cumsum(counted, axis=0) - counted
    slot_ids = lax.broadcasted_iota(jnp.int32, (1, 1, slot_count), 2)
    placed = (counted[:, :, None] == 1) & (before[:, :, None] == slot_ids)
    placed = placed.reshape(tok_count, row_count, per_row, slot_count)
    shares = (
        placed.astype(jnp.float32) * weighted.reshape(tok_count, row_count, per_row)[:, :, :, None]
    )
    place_bf = placed.astype(jnp.bfloat16)
    outgoing = jnp.einsum(
        "trjm,td->jrmd", place_bf, tokens, preferred_element_type=jnp.float32
    ).astype(jnp.bfloat16)
    share_out = jnp.transpose(shares, (2, 1, 3, 0)).astype(jnp.bfloat16)
    arrived, arrived_share, arrived_dither = (
        lax.all_to_all(outgoing, "row", split_axis=1, concat_axis=1, tiled=True),
        lax.all_to_all(share_out, "row", split_axis=1, concat_axis=1, tiled=True),
        lax.all_to_all(dither, "row", split_axis=1, concat_axis=1, tiled=True),
    )
    fanned = jnp.broadcast_to(arrived[:, None], (per_row, pieces) + arrived.shape[1:])
    fanned = fanned.reshape((col_count,) + arrived.shape[1:])
    returned = lax.all_to_all(
        expert_apply(
            lax.all_to_all(fanned, "col", split_axis=0, concat_axis=0, tiled=True),
            gate_proj[0, 0],
            up_proj[0, 0],
            down_proj[0, 0],
        ),
        "col",
        split_axis=0,
        concat_axis=0,
        tiled=True,
    )
    merged = jnp.sum(
        returned.reshape(per_row, pieces, row_count, slot_count, model_width).astype(jnp.float32),
        axis=1,
    )
    combined = jnp.einsum(
        "jrmt,jrmd->trd", arrived_share.astype(jnp.float32), merged, precision=lax.Precision.HIGHEST
    )
    spread = 0.125 * jnp.max(jnp.abs(combined), axis=2, keepdims=True)
    rounded = (combined + spread * (arrived_dither.astype(jnp.float32) - 0.5)).astype(jnp.bfloat16)
    collected = lax.all_to_all(rounded, "row", split_axis=1, concat_axis=1, tiled=True)
    return jnp.sum(collected.astype(jnp.float32), axis=1).astype(jnp.bfloat16)


N = 4
SLOTS = 3
BLOCKS = N * N
ROWS = BLOCKS * 4
EARLY = 1
HELD = 2
PACKED = N * SLOTS * N


def pack_kernel(tok_ref, ids_ref, share_ref, _, out_ref, ids_here, share_here, sem):
    width = tok_ref.shape[1]
    copies = [
        pltpu.make_async_copy(ids_ref, ids_here, sem.at[0]),
        pltpu.make_async_copy(share_ref, share_here, sem.at[1]),
        pltpu.make_async_copy(tok_ref, out_ref.at[:, pl.ds(0, width)], sem.at[2]),
    ]
    for c in copies:
        c.start()
    for c in copies:
        c.wait()
    tail = jnp.concatenate(
        [
            ids_here[...].astype(jnp.float32),
            share_here[...].astype(jnp.float32),
            jnp.zeros((4, LANES - 16), jnp.float32),
        ],
        axis=1,
    )
    out_ref[:, width:] = tail.astype(jnp.bfloat16)


def stack_kernel(*refs):
    out_ref, mark_ref = refs[-2:]
    mark_ref[...] = jnp.zeros_like(mark_ref)
    parts = [r[...].astype(jnp.float32) for r in refs[:4]]
    out_ref[...] = jnp.concatenate(parts, axis=0).astype(jnp.bfloat16)


def up_copy(up_ref, buf, sem, j, first):
    return pltpu.make_async_copy(
        up_ref.at[:, pl.ds(j * PAIR, PAIR)], buf.at[(j - first) % buf.shape[0]], sem.at[j]
    )


def fill_kernel(up_ref, _, buf, sem):
    copies = [up_copy(up_ref, buf, sem, j, 0) for j in range(buf.shape[0])]
    for c in copies:
        c.start()
    for c in copies:
        c.wait()


def routing(meta, me_row, me_col):
    ids, share = meta[:, :8], meta[:, 8:16]
    at = lax.broadcasted_iota(jnp.int32, (ROWS, ROWS), 0)
    to = lax.broadcasted_iota(jnp.int32, (ROWS, ROWS), 1)
    earlier = ((at // 4 == to // 4) & (to < at)).astype(jnp.bfloat16)
    found, rank, weight = [], [], []
    for k in range(N):
        expert = (me_row * N + (me_col ^ k)).astype(jnp.float32)
        hit = (ids == expert).astype(jnp.float32)
        found.append(jnp.sum(hit, axis=1, keepdims=True))
        weight.append(jnp.sum(hit * share, axis=1, keepdims=True))
    lanes = jnp.concatenate(found + [jnp.zeros((ROWS, LANES - N), jnp.float32)], axis=1)
    rank = jnp.dot(earlier, lanes.astype(jnp.bfloat16), preferred_element_type=jnp.float32)
    return found, rank, weight


def store_outs(value, outs, lo):
    width = value.shape[1]
    for k in range(N):
        for s in range(SLOTS):
            at = (k * SLOTS + s) * N
            outs[k][s, :, lo : lo + width] = value[at : at + N].astype(jnp.bfloat16)


def hidden_kernel(blocks, *refs):
    pieces = refs[:4]
    gate_ref, up_ref, down_ref, early_ref = refs[4:8]
    outs, hid_ref, mix_ref = refs[8:12], refs[12], refs[13]
    x_ref, h_ref, buf, piece_sem, fill_sem, down_sem = refs[14:]
    early = early_ref.shape[0]
    width = gate_ref.shape[0]
    deep = down_ref.shape[0]
    steps = deep // PAIR
    bring = [
        pltpu.make_async_copy(pieces[q], x_ref.at[pl.ds(q * 16, 16)], piece_sem.at[q])
        for q in range(N)
    ]
    for c in bring:
        c.start()
    for j in range(early, early + buf.shape[0]):
        up_copy(up_ref, buf, fill_sem, j, early).start()
    x_ref[ROWS:, :] = jnp.zeros((x_ref.shape[0] - ROWS, x_ref.shape[1]), x_ref.dtype)
    for c in bring:
        c.wait()

    def down_place(b):
        slot = (steps - early + b // 3) % buf.shape[0]
        return buf.at[slot, pl.ds(b % 3 * deep, deep)]

    def down_copy(b):
        return pltpu.make_async_copy(
            down_ref.at[:, pl.ds(b * PAIR, PAIR)], down_place(b), down_sem.at[b]
        )

    def load_next(used):
        j = used + early + buf.shape[0]
        if j < steps:
            up_copy(up_ref, buf, fill_sem, j, early).start()
            return
        first = 3 * (j - steps)
        for b in range(first, min(first + 3, blocks)):
            down_copy(b).start()

    for j in range(steps):
        at = pl.ds(j * PAIR, PAIR)
        g = jnp.dot(x_ref[:, :width], gate_ref[:, at], preferred_element_type=jnp.float32)[:ROWS]
        if j >= early:
            up_copy(up_ref, buf, fill_sem, j, early).wait()
        right = early_ref[j] if j < early else buf[(j - early) % buf.shape[0]]
        u = jnp.dot(x_ref[:, :width], right, preferred_element_type=jnp.float32)[:ROWS]
        h_ref[:, at] = (g / (1.0 + jnp.exp(-g)) * u).astype(jnp.bfloat16)
        if j >= early:
            load_next(j - early)

    meta = x_ref[:ROWS, width:].astype(jnp.float32)
    found, rank, weight = routing(meta, lax.axis_index("row"), lax.axis_index("col"))
    m_at = lax.broadcasted_iota(jnp.int32, (ROWS, PACKED), 0)
    c_at = lax.broadcasted_iota(jnp.int32, (ROWS, PACKED), 1)
    same = (m_at // 16 == c_at % 4) & ((m_at // 4) % 4 == c_at // 12)
    slot = ((c_at // 4) % 3).astype(jnp.float32)
    take = jnp.where(same & (found[0] > 0) & (rank[:, 0:1] == slot), 1.0, 0.0)
    hid = lax.dot_general(
        take.astype(jnp.bfloat16),
        h_ref[...],
        (((0,), (0,)), ((), ())),
        preferred_element_type=jnp.float32,
    )
    hid_ref[...] = hid.astype(jnp.bfloat16)
    mix = jnp.zeros((ROWS, PACKED), jnp.float32)
    for k in range(N):
        here = (c_at // 12 == k) & (m_at // 16 == c_at % 4)
        mix = jnp.where(here & (found[k] > 0) & (rank[:, k : k + 1] == slot), weight[k], mix)
    for q in range(N):
        mix_ref[q * 4 : q * 4 + 4, :] = mix[q * 16 : q * 16 + 4]
    for b in range(blocks):
        down_copy(b).wait()
        value = jnp.dot(
            hid_ref[...],
            down_place(b)[...],
            preferred_element_type=jnp.float32,
        )
        store_outs(value, outs, b * PAIR)
        if b % 3 == 2:
            load_next(steps - early + b // 3)


def down_kernel(first, last, hid_from, down_ref, *refs):
    outs, buf, hid_ref, sem, hid_sem = refs[:4], refs[4], refs[5], refs[6], refs[7]
    bring = pltpu.make_async_copy(hid_from, hid_ref, hid_sem)
    bring.start()
    cuts = [(i * PAIR, PAIR) for i in range(last - first - 1)]
    cuts += [((last - first) * PAIR - n * COLS, COLS) for n in (2, 1)]
    copies = []
    for i, (lo, wide) in enumerate(cuts):
        into = buf.at[lo // PAIR, :, pl.ds(lo % PAIR, wide)]
        copies.append(
            pltpu.make_async_copy(down_ref.at[:, pl.ds(first * PAIR + lo, wide)], into, sem.at[i])
        )
    for c in copies:
        c.start()
    bring.wait()
    for (lo, wide), c in zip(cuts, copies):
        c.wait()
        right = buf[lo // PAIR, :, lo % PAIR : lo % PAIR + wide]
        value = jnp.dot(hid_ref[...], right, preferred_element_type=jnp.float32)
        store_outs(value, outs, lo)


def merge_kernel(mix_ref, *refs):
    ins, outs = refs[:4], refs[-4:]
    got = jnp.concatenate(
        [ins[k][s].astype(jnp.float32) for k in range(N) for s in range(SLOTS)], axis=0
    ).astype(jnp.bfloat16)
    value = jnp.dot(
        mix_ref[...].astype(jnp.bfloat16), got, preferred_element_type=jnp.float32
    )
    for q in range(N):
        outs[q][...] = value[q * 4 : q * 4 + 4].astype(jnp.bfloat16)


def draw_kernel(dither_ref, _, out_ref):
    draw = dither_ref[...].astype(jnp.float32)
    at = lax.broadcasted_iota(jnp.int32, draw.shape, 1)
    for q in range(N):
        mine = jnp.where(at == (lax.axis_index("row") ^ q), draw, 0.0)
        out_ref[q] = (jnp.sum(mine, axis=1) - 0.5).astype(out_ref.dtype)


def final_kernel(chunks, draw_ref, *refs):
    ins, out_ref = refs[:-1], refs[-1]
    total, ends = [None] * chunks, [0]
    for c in range(chunks):
        ends.append(ends[-1] + ins[c * N].shape[1])
    for q in range(N):
        part = [ins[c * N + q][...].astype(jnp.float32) for c in range(chunks)]
        peak = [jnp.max(jnp.abs(p), axis=1, keepdims=True) for p in part]
        spread = 0.125 * functools.reduce(jnp.maximum, peak)
        for c in range(chunks):
            term = part[c] + spread * draw_ref[q, :, ends[c] : ends[c + 1]]
            total[c] = term if q == 0 else total[c] + term
    for c in range(chunks):
        out_ref[:, ends[c] : ends[c + 1]] = total[c].astype(jnp.bfloat16)


def local_grid(tokens, expert_ids, route_weight, dither, gate_proj, up_proj, down_proj):
    gate, up, down = gate_proj[0, 0], up_proj[0, 0], down_proj[0, 0]
    width, wide = gate.shape
    deep = down.shape[0]
    bf = jnp.bfloat16
    shape = jax.ShapeDtypeStruct
    anyw = pl.BlockSpec(memory_space=pl.ANY)
    pin = lambda a: pltpu.with_memory_space_constraint(a, pltpu.VMEM)

    packed = pl.pallas_call(
        pack_kernel,
        out_shape=shape((4, width + LANES), bf),
        in_specs=[HBM] * 4,
        out_specs=VMEM,
        scratch_shapes=[
            pltpu.VMEM((4, 8), jnp.int32),
            pltpu.VMEM((4, 8), bf),
            pltpu.SemaphoreType.DMA((3,)),
        ],
        compiler_params=params(6),
        name="pack",
    )(*(pltpu.with_memory_space_constraint(a, pltpu.HBM) for a in (tokens, expert_ids, route_weight, up)))
    near = [packed] + [lax.ppermute(packed, "col", flip(N, k)) for k in (1, 2, 3)]

    hbm = lambda a: pltpu.with_memory_space_constraint(a, pltpu.HBM)
    own, mark = pl.pallas_call(
        stack_kernel,
        out_shape=[shape((16, width + LANES), bf), shape((8, LANES), jnp.float32)],
        in_specs=[VMEM] * 4 + [HBM],
        out_specs=[VMEM] * 2,
        compiler_params=params(6),
        name="stack",
    )(*near, hbm(up))
    by_core = lax.ppermute(own, "row", flip(N, 1))
    by_x = lax.ppermute(own, "row", flip(N, 2))
    early = pl.pallas_call(
        fill_kernel,
        out_shape=pltpu.VMEM((EARLY, width, PAIR), bf),
        in_specs=[HBM, anyw],
        out_specs=VMEM,
        scratch_shapes=[pltpu.SemaphoreType.DMA((EARLY,))],
        compiler_params=params(SCOPED),
        cost_estimate=cost(0, EARLY * width * PAIR * 2),
        name="fill",
    )(hbm(up), mark)
    by_x, early = lax.optimization_barrier((by_x, early))
    by_both = lax.ppermute(by_x, "row", flip(N, 1))

    chunks = (8, 6)
    outs = [shape((SLOTS, N, n * PAIR), bf) for n in chunks]
    first = pl.pallas_call(
        functools.partial(hidden_kernel, chunks[0]),
        out_shape=[outs[0]] * 4 + [pltpu.VMEM((PACKED, wide), bf), pltpu.VMEM((16, PACKED), jnp.float32)],
        in_specs=[anyw] * 4 + [VMEM] + [HBM] * 2 + [VMEM],
        out_specs=[VMEM] * 6,
        scratch_shapes=[
            pltpu.VMEM((2 * ROWS, width + LANES), bf),
            pltpu.VMEM((ROWS, wide), bf),
            pltpu.VMEM((HELD, width, PAIR), bf),
            pltpu.SemaphoreType.DMA((N,)),
            pltpu.SemaphoreType.DMA((wide // PAIR,)),
            pltpu.SemaphoreType.DMA((chunks[0],)),
        ],
        compiler_params=params(SCOPED),
        cost_estimate=cost(2 * ROWS * width * wide * 3, 40 * MIB),
        name="hidden",
    )(own, by_core, by_x, by_both, pin(gate), hbm(up), hbm(down), pin(early))
    hid, mix = first[4:6]
    parts = [first[:4]]
    parts.append(
        pl.pallas_call(
            functools.partial(down_kernel, chunks[0], chunks[0] + chunks[1]),
            out_shape=[outs[1]] * 4,
            in_specs=[anyw, HBM],
            out_specs=[VMEM] * 4,
            scratch_shapes=[
                pltpu.VMEM((chunks[1], deep, PAIR), bf),
                pltpu.VMEM((PACKED, wide), bf),
                pltpu.SemaphoreType.DMA((chunks[1] + 1,)),
                pltpu.SemaphoreType.DMA,
            ],
            compiler_params=params(28),
            cost_estimate=cost(2 * ROWS * width * wide, 10 * MIB),
            name="down",
        )(hid, pltpu.with_memory_space_constraint(down, pltpu.HBM))
    )
    finals = []
    after = []
    for c, part in enumerate(parts):
        got = [part[0]] + [lax.ppermute(part[k], "col", flip(N, k)) for k in (1, 2, 3)]
        value = pl.pallas_call(
            merge_kernel,
            out_shape=[shape((4, chunks[c] * PAIR), bf)] * 4,
            in_specs=[VMEM] * 5 + [anyw] * len(after),
            out_specs=[VMEM] * 4,
            compiler_params=params(6),
            cost_estimate=cost(0, 8 * MIB),
            name="merge",
        )(mix, *got, *after)
        if c == 0:
            draws = pl.pallas_call(
                draw_kernel,
                out_shape=shape((N, 4, width), jnp.float32),
                in_specs=[VMEM, anyw],
                out_specs=VMEM,
                compiler_params=params(6),
                cost_estimate=cost(0, 8 * MIB),
                name="draws",
            )(dither, value[0])
        sent = [lax.ppermute(value[q], "row", flip(N, q)) for q in (1, 2, 3)]
        finals += [value[0]] + sent
        after = [draws] + sent
    return pl.pallas_call(
        functools.partial(final_kernel, len(chunks)),
        out_shape=shape((4, width), bf),
        in_specs=[VMEM] * (1 + len(finals)),
        out_specs=VMEM,
        compiler_params=params(6),
        name="final",
    )(draws, *finals)


def solution(mesh):
    def local(tokens, expert_ids, route_weight, dither, gate_proj, up_proj, down_proj):
        grid = (mesh.shape["row"], mesh.shape["col"]) == (N, N)
        whole_expert = gate_proj.shape[3] == FF and tokens.shape[0] == 4
        pick = local_grid if grid and whole_expert else local_any
        return pick(tokens, expert_ids, route_weight, dither, gate_proj, up_proj, down_proj)

    return jax.shard_map(
        local,
        mesh=mesh,
        in_specs=(
            P(("groups", "row", "col"), None),
            P(("groups", "row", "col"), None),
            P(("groups", "row", "col"), None),
            P(("groups", "row", "col"), None, None),
            P("row", "col", None, None),
            P("row", "col", None, None),
            P("row", "col", None, None),
        ),
        out_specs=P(("groups", "row", "col"), None),
        check_vma=False,
    )
```
